256 devices in a mesh: section: 8 (over z), tp: 32 (over x, y, core).
Axes of the slice: x: 4, y: 4, z: 8, core: 2. Of those that a mesh axis runs over, the one named last changes fastest.
Arguments:
- section_inputs: bfloat16 [8, 192, 4096], P('section', None, 'tp'), may hold values from -6 to 6
- top_gradient: float32 [192, 4096], P(None, 'tp'), may hold values from -6 to 6
- gate_weight: bfloat16 [8, 4096, 14336], P('section', None, 'tp'), may hold values from -0.09375 to 0.09375
- up_weight: bfloat16 [8, 4096, 14336], P('section', None, 'tp'), may hold values from -0.09375 to 0.09375
- down_weight: bfloat16 [8, 14336, 4096], P('section', 'tp'), may hold values from -0.046875 to 0.046875
Outputs:
- section_grads: float32 [8, 192, 4096], P('section', None, 'tp')
- kept_scores: float32 [8, 3584, 4096], P('section', 'tp')
The draws below stay inside these ranges and needn't reach their ends.
All inputs are finite; a program needn't handle non-finite values.
Results may differ from the reference program's by a relative error of at most 0.04.
Values may be sent and summed in bfloat16 or wider, within the bound.
A program may use at most 128 MiB of HBM per device.

```python
import jax
import jax.numpy as jnp
from jax import lax

D = 4096
FF = 14336
SEQ = 64
SAMPLES = 3
ROWS = 192
N_SECTION = 8
N_TP = 32


def block_scale(stream_key, shape, shards, smallest, top_value):
    def one(dim, blocks):
        heights = jax.random.uniform(jax.random.fold_in(jax.random.fold_in(stream_key, 6), dim), (blocks,), jnp.float32, smallest / len(shards), top_value / len(shards))
        return jnp.repeat(jnp.exp(heights), shape[dim] // blocks).reshape((-1,) + (1,) * (len(shape) - dim - 1))

    gain = one(*shards[0])
    for cut in shards[1:]:
        gain = gain * one(*cut)
    return gain


def centred(rng, shape, deviation, most, split=(), dtype=jnp.bfloat16):
    values = jax.random.normal(rng, shape, jnp.float32) * deviation
    if len(split) > 0:
        values = block_scale(rng, shape, split, -0.22, 0.18) * values
    return jnp.clip(values, min=-most, max=most).astype(dtype)


def setup_inputs(seed: int = 0) -> dict:
    arg_keys = jax.random.split(jax.random.key(seed), 6)
    section_inputs = centred(arg_keys[0], (N_SECTION, ROWS, D), 1.0, 6.0, ((0, 8), (2, 32)))
    top_gradient = centred(arg_keys[1], (ROWS, D), 1.0, 6.0, ((1, 32),), jnp.float32)
    gate_weight = centred(arg_keys[2], (N_SECTION, D, FF), D ** -0.5, 0.09375, ((0, 8), (2, 32)))
    up_weight = centred(arg_keys[3], (N_SECTION, D, FF), D ** -0.5, 0.09375, ((0, 8), (2, 32)))
    down_weight = centred(arg_keys[4], (N_SECTION, FF, D), FF ** -0.5, 0.046875, ((0, 8), (1, 32)))
    return {"section_inputs": section_inputs, "top_gradient": top_gradient, "gate_weight": gate_weight, "up_weight": up_weight, "down_weight": down_weight}


def reference(section_inputs, top_gradient, gate_weight, up_weight, down_weight):
    grad_out = top_gradient.astype(jnp.float32)
    grads_list = [None] * N_SECTION
    kept_list = [None] * N_SECTION
    group_width = FF // N_TP
    for section in reversed(range(N_SECTION)):
        section_rows = section_inputs[section]
        pre_gate = jnp.dot(section_rows, gate_weight[section], preferred_element_type=jnp.float32)
        pre_up = jnp.dot(section_rows, up_weight[section], preferred_element_type=jnp.float32)
        silu_gate = jax.nn.silu(pre_gate)
        hidden = (silu_gate * pre_up).astype(jnp.bfloat16)
        sigmoid_gate = jax.nn.sigmoid(pre_gate)
        slope = sigmoid_gate * (1.0 + pre_gate * (1.0 - sigmoid_gate))
        grad16 = grad_out.astype(jnp.bfloat16)
        hidden_grad = jnp.dot(grad16, down_weight[section].T, preferred_element_type=jnp.float32)
        grad_gate = (hidden_grad * (pre_up * slope)).astype(jnp.bfloat16)
        grad_up = (hidden_grad * silu_gate).astype(jnp.bfloat16)
        gate_blocks = grad_gate.astype(jnp.float32).reshape(ROWS, N_TP, group_width)
        up_blocks = grad_up.astype(jnp.float32).reshape(ROWS, N_TP, group_width)
        gate_cols = gate_weight[section].astype(jnp.float32).reshape(D, N_TP, group_width)
        up_cols = up_weight[section].astype(jnp.float32).reshape(D, N_TP, group_width)
        terms = jnp.einsum('rjf,djf->jrd', gate_blocks, gate_cols) + jnp.einsum('rjf,djf->jrd', up_blocks, up_cols)
        rounded = lax.optimization_barrier(terms.astype(jnp.bfloat16))
        input_term = lax.optimization_barrier(jnp.sum(rounded.astype(jnp.float32), axis=0))
        result = grad_out + input_term
        grads_list[section] = result
        squares = jnp.zeros((FF, D), jnp.float32)
        for sample in range(SAMPLES):
            hidden_rows = hidden[sample * SEQ:(sample + 1) * SEQ]
            grad_rows = grad16[sample * SEQ:(sample + 1) * SEQ]
            weight_grad = jnp.dot(hidden_rows.T, grad_rows, preferred_element_type=jnp.float32)
            squares = squares + weight_grad * weight_grad
        score = jnp.abs(down_weight[section].astype(jnp.float32)) * jnp.sqrt(squares)
        ordered = jnp.sort(score.reshape(FF // 4, 4, D), axis=1)
        kept_list[section] = ordered[:, 2] + ordered[:, 3]
        grad_out = result
    return (jnp.stack(grads_list), jnp.stack(kept_list))
```

```python
import functools

import jax
import jax.numpy as jnp
from jax import lax
from jax.experimental import pallas as pl
from jax.experimental.pallas import tpu as pltpu
from jax.sharding import PartitionSpec as P

SAMPLES = 3
CHUNK = 128
ROWS_PER_STEP = 32
MESH = pl.DeviceIdType.MESH
BF16 = jnp.bfloat16
F32 = jnp.float32


def grid_sides(chips):
    side = 1
    while side * side < chips:
        side *= 2
    return chips // side, side


def ring_distance(step, size):
    return min(step, size - step)


def chip_offsets(nx, ny):
    offsets = [(dx, dy) for dx in range(nx) for dy in range(ny)]
    return sorted(offsets, key=lambda o: -(ring_distance(o[0], nx) + ring_distance(o[1], ny)))


def kernel(
    sections,
    chips,
    rows,
    step_rows,
    units,
    x_ref,
    top_ref,
    wg_hbm,
    wu_hbm,
    wd_hbm,
    grad_ref,
    kept_ref,
    w_gate,
    w_up,
    w_down,
    w_own,
    down_t,
    both_t,
    x_all,
    g_all,
    g_other,
    top16,
    result16,
    send_buf,
    recv_buf,
    part_mine,
    part_other,
    pre_mine,
    pre_other,
    factor_gate,
    factor_up,
    hidden_t,
    load_sem,
    swap_sem,
    x_sem,
    pre_sem,
    gather_sem,
    below_sem,
    part_sem,
    forward_sem,
    term_sem,
):
    nx, ny = grid_sides(chips)
    offsets = chip_offsets(nx, ny)
    steps = rows // step_rows
    half = chips * CHUNK
    section = lax.axis_index("section")
    index = lax.axis_index("tp")
    chip, core = index // 2, lax.rem(index, 2)
    other = 1 - core
    chip_x, chip_y = chip // ny, lax.rem(chip, ny)
    places = [lax.rem(chip_x + dx, nx) * ny + lax.rem(chip_y + dy, ny) for dx, dy in offsets]
    sibling = (section, 2 * chip + other)
    above = lax.rem(section + 1, sections)
    below = lax.rem(section + sections - 1, sections)
    is_top = section == sections - 1
    is_last = section == 0

    pltpu.make_async_copy(wg_hbm.at[:, core], w_gate.at[core], load_sem.at[0]).start()
    pltpu.make_async_copy(wu_hbm.at[:, core], w_up.at[core], load_sem.at[1]).start()
    for k in range(chips):
        mine = pl.ds(pl.multiple_of((2 * k + core) * CHUNK, CHUNK), CHUNK)
        pltpu.make_async_copy(
            wd_hbm.at[:, mine], w_down.at[core, :, pl.ds(k * CHUNK, CHUNK)], load_sem.at[2]
        ).start()
    pltpu.make_async_copy(wd_hbm, w_own, load_sem.at[3]).start()

    barrier = pltpu.get_barrier_semaphore()
    pl.semaphore_signal(barrier, inc=1, device_id=sibling, device_id_type=MESH)
    for place in places[:-1]:
        pl.semaphore_signal(
            barrier, inc=1, device_id=(section, 2 * place + core), device_id_type=MESH
        )

    @pl.when(jnp.logical_not(is_top))
    def _():
        for place in places:
            pl.semaphore_signal(
                barrier, inc=1, device_id=(above, 2 * place + core), device_id_type=MESH
            )

    @pl.when(jnp.logical_not(is_last))
    def _():
        for place in places:
            pl.semaphore_signal(
                barrier, inc=1, device_id=(below, 2 * place + core), device_id_type=MESH
            )

    top16[...] = top_ref[...].astype(BF16)
    neighbours = (
        chips
        + jnp.where(is_top, 0, chips)
        + jnp.where(is_last, 0, chips)
    )
    pl.semaphore_wait(barrier, neighbours)

    def spread_top(step):
        at = pl.ds(step * step_rows, step_rows)
        for place in places[:-1]:
            pltpu.make_async_remote_copy(
                src_ref=top16.at[at],
                dst_ref=g_all.at[chip, at],
                send_sem=below_sem.at[steps + step],
                recv_sem=gather_sem.at[step],
                device_id=(section, 2 * place + core),
                device_id_type=MESH,
            ).start()
        pltpu.make_async_copy(top16.at[at], g_all.at[chip, at], gather_sem.at[step]).start()

    @pl.when(is_top)
    def _():
        spread_top(0)

    for n, (source, target) in enumerate(((wg_hbm, w_gate), (wu_hbm, w_up))):
        pltpu.make_async_remote_copy(
            src_ref=source.at[:, other],
            dst_ref=target.at[core],
            send_sem=swap_sem.at[n],
            recv_sem=swap_sem.at[3 + n],
            device_id=sibling,
            device_id_type=MESH,
        ).start()
    for place in places[:-1]:
        pltpu.make_async_remote_copy(
            src_ref=x_ref,
            dst_ref=x_all.at[chip],
            send_sem=x_sem.at[0],
            recv_sem=x_sem.at[1],
            device_id=(section, 2 * place + core),
            device_id_type=MESH,
        ).start()
    pltpu.make_async_copy(x_ref, x_all.at[chip], x_sem.at[1]).start()
    for k in range(chips):
        theirs = pl.ds(pl.multiple_of((2 * k + other) * CHUNK, CHUNK), CHUNK)
        pltpu.make_async_remote_copy(
            src_ref=wd_hbm.at[:, theirs],
            dst_ref=w_down.at[core, :, pl.ds(k * CHUNK, CHUNK)],
            send_sem=swap_sem.at[2],
            recv_sem=swap_sem.at[5],
            device_id=sibling,
            device_id_type=MESH,
        ).start()

    @pl.when(is_top)
    def _():
        for step in range(1, steps):
            spread_top(step)

    def wait(ref, sem):
        pltpu.make_async_copy(ref, ref, sem).wait()

    wait(w_gate.at[core], load_sem.at[0])
    wait(w_up.at[core], load_sem.at[1])
    wait(x_all, x_sem.at[1])
    wait(w_gate.at[other], swap_sem.at[3])
    wait(w_up.at[other], swap_sem.at[4])
    x_rows = jnp.concatenate([x_all[k] for k in range(chips)], axis=1)
    for n, weight in enumerate((w_gate, w_up)):
        for h in range(2):
            pre_mine[n, h] = jnp.dot(
                x_rows, weight[h].reshape(half, units), preferred_element_type=F32
            )
        pltpu.make_async_remote_copy(
            src_ref=pre_mine.at[n],
            dst_ref=pre_other.at[n],
            send_sem=pre_sem.at[n],
            recv_sem=pre_sem.at[2 + n],
            device_id=sibling,
            device_id_type=MESH,
        ).start()

    for n, weight in enumerate((w_gate, w_up)):
        for h in range(2):
            for t, place in enumerate(places):
                both_t[pl.ds((2 * n + h) * units, units), pl.ds(t * CHUNK, CHUNK)] = weight[h, place].T
    wait(w_down.at[core], load_sem.at[2])
    wait(w_down.at[other], swap_sem.at[5])
    for k in range(chips):
        at = pl.ds(k * CHUNK, CHUNK)
        down_t[at, :] = jnp.concatenate([w_down[0, :, at], w_down[1, :, at]], axis=0).T

    fourth = units // 4
    to_place = lax.broadcasted_iota(jnp.int32, (units, units), 0)
    from_unit = lax.broadcasted_iota(jnp.int32, (units, units), 1)
    member = (
        (to_place >= fourth).astype(jnp.int32)
        + (to_place >= 2 * fourth).astype(jnp.int32)
        + (to_place >= 3 * fourth).astype(jnp.int32)
    )
    spread = (from_unit == 4 * (to_place - member * fourth) + member).astype(F32).astype(BF16)

    wait(pre_other.at[0], pre_sem.at[2])
    wait(pre_other.at[1], pre_sem.at[3])
    gates, ups = [], []
    for h in range(2):
        pre_gate = pre_mine[0, h] + pre_other[0, h]
        pre_up = pre_mine[1, h] + pre_other[1, h]
        sigmoid = jax.nn.sigmoid(pre_gate)
        silu = pre_gate * sigmoid
        gates.append(pre_up * (sigmoid * (1.0 + pre_gate * (1.0 - sigmoid))))
        ups.append(silu)
        hidden = (silu * pre_up).astype(BF16)

        @pl.when(core == h)
        def _():
            for sample in range(SAMPLES):
                some = hidden[sample * (rows // SAMPLES) : (sample + 1) * (rows // SAMPLES)]
                hidden_t[sample] = lax.dot_general(
                    spread, some, (((1,), (1,)), ((), ())), preferred_element_type=F32
                ).astype(BF16)

    factor_gate[...] = jnp.concatenate(gates, axis=1)
    factor_up[...] = jnp.concatenate(ups, axis=1)

    def rows_of(step):
        return pl.ds(pl.multiple_of(step * step_rows, step_rows), step_rows)

    def first(step):
        at = rows_of(step)
        wait(g_all.at[:, at], gather_sem.at[step])
        grads = jnp.concatenate([g_all[k, at, :] for k in range(chips)], axis=1)
        part_mine[at, :] = jnp.dot(grads, down_t[...], preferred_element_type=F32)
        pltpu.make_async_remote_copy(
            src_ref=part_mine.at[at],
            dst_ref=part_other.at[at],
            send_sem=part_sem.at[0, step],
            recv_sem=part_sem.at[1, step],
            device_id=sibling,
            device_id_type=MESH,
        ).start()
        pltpu.make_async_remote_copy(
            src_ref=g_all.at[:, at],
            dst_ref=g_other.at[:, at],
            send_sem=forward_sem.at[0, step],
            recv_sem=forward_sem.at[1, step],
            device_id=sibling,
            device_id_type=MESH,
        ).start()

    def second(step):
        at = rows_of(step)
        wait(part_other.at[at], part_sem.at[1, step])
        hidden_grad = part_mine[at, :] + part_other[at, :]
        both = jnp.concatenate(
            [
                (hidden_grad * factor_gate[at, :]).astype(BF16),
                (hidden_grad * factor_up[at, :]).astype(BF16),
            ],
            axis=1,
        )
        for pair in range(chips // 2):
            term = jnp.dot(
                both,
                both_t[:, pl.ds(2 * pair * CHUNK, 2 * CHUNK)],
                preferred_element_type=F32,
            ).astype(BF16)
            for t in (2 * pair, 2 * pair + 1):
                send_buf[t, at, :] = term[:, (t - 2 * pair) * CHUNK : (t - 2 * pair + 1) * CHUNK]
                if t < chips - 1:
                    pltpu.make_async_remote_copy(
                        src_ref=send_buf.at[t, at],
                        dst_ref=recv_buf.at[t, at],
                        send_sem=term_sem.at[0, step],
                        recv_sem=term_sem.at[1, step],
                        device_id=(section, 2 * places[t] + core),
                        device_id_type=MESH,
                    ).start()

    def third(step):
        at = rows_of(step)
        wait(recv_buf.at[:, at], term_sem.at[1, step])
        total = send_buf[chips - 1, at, :].astype(F32)
        for t in range(chips - 1):
            total = total + recv_buf[t, at, :].astype(F32)
        result = jnp.where(is_top, top_ref[at, :], g_all[chip, at, :].astype(F32)) + total
        grad_ref[at, :] = result
        result16[at, :] = result.astype(BF16)

        @pl.when(jnp.logical_not(is_last))
        def _():
            for place in places:
                pltpu.make_async_remote_copy(
                    src_ref=result16.at[at],
                    dst_ref=g_all.at[chip, at],
                    send_sem=below_sem.at[step],
                    recv_sem=gather_sem.at[step],
                    device_id=(below, 2 * place + core),
                    device_id_type=MESH,
                ).start()

    lag = 2

    @pl.loop(0, steps)
    def _(step):
        first(step)

        @pl.when(step >= lag)
        def _():
            third(step - lag)

        second(step)

    @pl.loop(steps - lag, steps)
    def _(step):
        third(step)

    wait(w_own, load_sem.at[3])

    @pl.loop(0, steps)
    def _(step):
        wait(g_other.at[:, rows_of(step)], forward_sem.at[1, step])

    per_sample = rows // SAMPLES

    @pl.loop(0, chips // 2)
    def _(pair):
        for grads, parity in ((g_all, core), (g_other, other)):
            blocks = [2 * pair, 2 * pair + 1]
            columns = [pl.ds(pl.multiple_of((2 * k + parity) * CHUNK, CHUNK), CHUNK) for k in blocks]
            squares = None
            for sample in range(SAMPLES):
                some = jnp.concatenate(
                    [grads[k, pl.ds(sample * per_sample, per_sample), :] for k in blocks], axis=1
                )
                weight_grad = jnp.dot(hidden_t[sample], some, preferred_element_type=F32)
                square = weight_grad * weight_grad
                squares = square if squares is None else squares + square
            weight = jnp.dot(
                spread,
                jnp.concatenate([w_own[:, c] for c in columns], axis=1),
                preferred_element_type=F32,
            )
            score = jnp.abs(weight) * jnp.sqrt(squares)
            a, b, c, d = [score[i * fourth : (i + 1) * fourth] for i in range(4)]
            high_ab, low_ab = jnp.maximum(a, b), jnp.minimum(a, b)
            high_cd, low_cd = jnp.maximum(c, d), jnp.minimum(c, d)
            best = jnp.maximum(high_ab, high_cd)
            next_best = jnp.maximum(jnp.minimum(high_ab, high_cd), jnp.maximum(low_ab, low_cd))
            kept = best + next_best
            for n in range(2):
                kept_ref[:, columns[n]] = kept[:, n * CHUNK : (n + 1) * CHUNK]

    wait(w_gate.at[core], swap_sem.at[0])
    wait(w_up.at[core], swap_sem.at[1])
    wait(w_down.at[core], swap_sem.at[2])
    wait(x_all.at[pl.ds(0, chips - 1)], x_sem.at[0])
    wait(pre_mine.at[0], pre_sem.at[0])
    wait(pre_mine.at[1], pre_sem.at[1])

    @pl.loop(0, steps)
    def _(step):
        at = rows_of(step)
        wait(part_mine.at[at], part_sem.at[0, step])
        wait(g_all.at[:, at], forward_sem.at[0, step])
        wait(recv_buf.at[:, at], term_sem.at[0, step])

        @pl.when(jnp.logical_not(is_last))
        def _():
            wait(g_all.at[:, at], below_sem.at[step])

        @pl.when(is_top)
        def _():
            wait(recv_buf.at[:, at], below_sem.at[steps + step])


def shards(sections, section_inputs, top_gradient, gate_weight, up_weight, down_weight):
    _, rows, width = section_inputs.shape
    _, model, units = gate_weight.shape
    chips = model // CHUNK // 2
    step_rows = ROWS_PER_STEP
    steps = rows // step_rows
    half = chips * CHUNK
    vmem = pl.BlockSpec(memory_space=pltpu.VMEM)
    hbm = pl.BlockSpec(memory_space=pl.ANY)
    dma = pltpu.SemaphoreType.DMA
    grads, kept = pl.pallas_call(
        functools.partial(kernel, sections, chips, rows, step_rows, units),
        out_shape=(
            jax.ShapeDtypeStruct((rows, width), F32),
            jax.ShapeDtypeStruct((units // 4, model), F32),
        ),
        in_specs=[vmem, vmem, hbm, hbm, hbm],
        out_specs=(vmem, vmem),
        scratch_shapes=[
            pltpu.VMEM((2, chips, CHUNK, units), BF16),
            pltpu.VMEM((2, chips, CHUNK, units), BF16),
            pltpu.VMEM((2, units, half), BF16),
            pltpu.VMEM((units, model), BF16),
            pltpu.VMEM((half, 2 * units), BF16),
            pltpu.VMEM((4 * units, half), BF16),
            pltpu.VMEM((chips, rows, CHUNK), BF16),
            pltpu.VMEM((chips, rows, CHUNK), BF16),
            pltpu.VMEM((chips, rows, CHUNK), BF16),
            pltpu.VMEM((rows, CHUNK), BF16),
            pltpu.VMEM((rows, CHUNK), BF16),
            pltpu.VMEM((chips, rows, CHUNK), BF16),
            pltpu.VMEM((chips - 1, rows, CHUNK), BF16),
            pltpu.VMEM((rows, 2 * units), F32),
            pltpu.VMEM((rows, 2 * units), F32),
            pltpu.VMEM((2, 2, rows, units), F32),
            pltpu.VMEM((2, 2, rows, units), F32),
            pltpu.VMEM((rows, 2 * units), F32),
            pltpu.VMEM((rows, 2 * units), F32),
            pltpu.VMEM((SAMPLES, units, rows // SAMPLES), BF16),
            dma((4,)),
            dma((6,)),
            dma((2,)),
            dma((4,)),
            dma((steps,)),
            dma((2 * steps,)),
            dma((2, steps)),
            dma((2, steps)),
            dma((2, steps)),
        ],
        compiler_params=pltpu.CompilerParams(
            collective_id=0, has_side_effects=True, vmem_limit_bytes=56 * 1024 * 1024
        ),
    )(
        section_inputs[0],
        top_gradient,
        gate_weight[0].reshape(chips, 2, CHUNK, units),
        up_weight[0].reshape(chips, 2, CHUNK, units),
        down_weight[0],
    )
    return (grads[None], kept[None])


def solution(mesh):
    in_specs = (
        P("section", None, "tp"),
        P(None, "tp"),
        P("section", None, "tp"),
        P("section", None, "tp"),
        P("section", "tp", None),
    )
    out_specs = (P("section", None, "tp"), P("section", "tp", None))
    body = functools.partial(shards, mesh.shape["section"])
    return jax.shard_map(body, mesh=mesh, in_specs=in_specs, out_specs=out_specs, check_vma=False)
```

```python
import functools

import jax
import jax.numpy as jnp
from jax import lax
from jax.experimental import pallas as pl
from jax.experimental.pallas import tpu as pltpu
from jax.sharding import PartitionSpec as P

SAMPLES = 3
CHUNK = 128
ROWS_PER_STEP = 32
MESH = pl.DeviceIdType.MESH
BF16 = jnp.bfloat16
F32 = jnp.float32


def grid_sides(chips):
    side = 1
    while side * side < chips:
        side *= 2
    return chips // side, side


def ring_distance(step, size):
    return min(step, size - step)


def chip_offsets(nx, ny):
    offsets = [(dx, dy) for dx in range(nx) for dy in range(ny)]
    return sorted(offsets, key=lambda o: -(ring_distance(o[0], nx) + ring_distance(o[1], ny)))


def kernel(
    sections,
    chips,
    rows,
    step_rows,
    units,
    x_ref,
    top_ref,
    wg_hbm,
    wu_hbm,
    wd_hbm,
    grad_ref,
    kept_ref,
    w_down,
    w_own,
    down_t,
    both_t,
    x_all,
    g_all,
    g_other,
    top16,
    result16,
    send_buf,
    recv_buf,
    part_mine,
    part_other,
    pre_mine,
    pre_other,
    factor_gate,
    factor_up,
    hidden_t,
    load_sem,
    swap_sem,
    x_sem,
    pre_sem,
    gather_sem,
    below_sem,
    part_sem,
    forward_sem,
    term_sem,
):
    nx, ny = grid_sides(chips)
    offsets = chip_offsets(nx, ny)
    steps = rows // step_rows
    half = chips * CHUNK
    section = lax.axis_index("section")
    index = lax.axis_index("tp")
    chip, core = index // 2, lax.rem(index, 2)
    other = 1 - core
    chip_x, chip_y = chip // ny, lax.rem(chip, ny)
    places = [lax.rem(chip_x + dx, nx) * ny + lax.rem(chip_y + dy, ny) for dx, dy in offsets]
    sibling = (section, 2 * chip + other)
    above = lax.rem(section + 1, sections)
    below = lax.rem(section + sections - 1, sections)
    is_top = section == sections - 1
    is_last = section == 0

    def columns_of(place, parity):
        return pl.ds(pl.multiple_of((2 * place + parity) * CHUNK, CHUNK), CHUNK)

    for n, source in enumerate((wg_hbm, wu_hbm)):
        for t, place in enumerate(places):
            pltpu.make_async_copy(
                source.at[:, columns_of(place, core)],
                both_t.at[n, core, :, pl.ds(t * CHUNK, CHUNK)],
                load_sem.at[n],
            ).start()
    for k in range(chips):
        pltpu.make_async_copy(
            wd_hbm.at[:, columns_of(k, core)],
            w_down.at[core, :, pl.ds(k * CHUNK, CHUNK)],
            load_sem.at[2],
        ).start()
    pltpu.make_async_copy(wd_hbm, w_own, load_sem.at[3]).start()

    barrier = pltpu.get_barrier_semaphore()
    pl.semaphore_signal(barrier, inc=1, device_id=sibling, device_id_type=MESH)
    for place in places[:-1]:
        pl.semaphore_signal(
            barrier, inc=1, device_id=(section, 2 * place + core), device_id_type=MESH
        )

    @pl.when(jnp.logical_not(is_top))
    def _():
        for place in places:
            pl.semaphore_signal(
                barrier, inc=1, device_id=(above, 2 * place + core), device_id_type=MESH
            )

    @pl.when(jnp.logical_not(is_last))
    def _():
        for place in places:
            pl.semaphore_signal(
                barrier, inc=1, device_id=(below, 2 * place + core), device_id_type=MESH
            )

    top16[...] = top_ref[...].astype(BF16)
    neighbours = (
        chips
        + jnp.where(is_top, 0, chips)
        + jnp.where(is_last, 0, chips)
    )
    pl.semaphore_wait(barrier, neighbours)

    def spread_top(step):
        at = pl.ds(step * step_rows, step_rows)
        for place in places[:-1]:
            pltpu.make_async_remote_copy(
                src_ref=top16.at[at],
                dst_ref=g_all.at[chip, at],
                send_sem=below_sem.at[steps + step],
                recv_sem=gather_sem.at[step],
                device_id=(section, 2 * place + core),
                device_id_type=MESH,
            ).start()
        pltpu.make_async_copy(top16.at[at], g_all.at[chip, at], gather_sem.at[step]).start()

    @pl.when(is_top)
    def _():
        spread_top(0)

    for n, source in enumerate((wg_hbm, wu_hbm)):
        for t, place in enumerate(places):
            pltpu.make_async_remote_copy(
                src_ref=source.at[:, columns_of(place, other)],
                dst_ref=both_t.at[n, core, :, pl.ds(t * CHUNK, CHUNK)],
                send_sem=swap_sem.at[n],
                recv_sem=swap_sem.at[3 + n],
                device_id=sibling,
                device_id_type=MESH,
            ).start()
    for place in places[:-1]:
        pltpu.make_async_remote_copy(
            src_ref=x_ref,
            dst_ref=x_all.at[chip],
            send_sem=x_sem.at[0],
            recv_sem=x_sem.at[1],
            device_id=(section, 2 * place + core),
            device_id_type=MESH,
        ).start()
    pltpu.make_async_copy(x_ref, x_all.at[chip], x_sem.at[1]).start()
    for k in range(chips):
        pltpu.make_async_remote_copy(
            src_ref=wd_hbm.at[:, columns_of(k, other)],
            dst_ref=w_down.at[core, :, pl.ds(k * CHUNK, CHUNK)],
            send_sem=swap_sem.at[2],
            recv_sem=swap_sem.at[5],
            device_id=sibling,
            device_id_type=MESH,
        ).start()

    @pl.when(is_top)
    def _():
        for step in range(1, steps):
            spread_top(step)

    def wait(ref, sem):
        pltpu.make_async_copy(ref, ref, sem).wait()

    wait(x_all, x_sem.at[1])
    x_rows = jnp.concatenate([x_all[place] for place in places], axis=1)
    for n in range(2):
        wait(both_t.at[n, core], load_sem.at[n])
        wait(both_t.at[n, other], swap_sem.at[3 + n])
        for h in range(2):
            pre_mine[n, h] = lax.dot_general(
                x_rows, both_t[n, h], (((1,), (1,)), ((), ())), preferred_element_type=F32
            )
        pltpu.make_async_remote_copy(
            src_ref=pre_mine.at[n],
            dst_ref=pre_other.at[n],
            send_sem=pre_sem.at[n],
            recv_sem=pre_sem.at[2 + n],
            device_id=sibling,
            device_id_type=MESH,
        ).start()

    wait(w_down.at[core], load_sem.at[2])
    wait(w_down.at[other], swap_sem.at[5])
    for k in range(chips):
        at = pl.ds(k * CHUNK, CHUNK)
        down_t[at, :] = jnp.concatenate([w_down[0, :, at], w_down[1, :, at]], axis=0).T

    fourth = units // 4
    to_place = lax.broadcasted_iota(jnp.int32, (units, units), 0)
    from_unit = lax.broadcasted_iota(jnp.int32, (units, units), 1)
    member = (
        (to_place >= fourth).astype(jnp.int32)
        + (to_place >= 2 * fourth).astype(jnp.int32)
        + (to_place >= 3 * fourth).astype(jnp.int32)
    )
    spread = (from_unit == 4 * (to_place - member * fourth) + member).astype(F32).astype(BF16)

    wait(pre_other.at[0], pre_sem.at[2])
    wait(pre_other.at[1], pre_sem.at[3])
    gates, ups = [], []
    for h in range(2):
        pre_gate = pre_mine[0, h] + pre_other[0, h]
        pre_up = pre_mine[1, h] + pre_other[1, h]
        sigmoid = jax.nn.sigmoid(pre_gate)
        silu = pre_gate * sigmoid
        gates.append(pre_up * (sigmoid * (1.0 + pre_gate * (1.0 - sigmoid))))
        ups.append(silu)
        hidden = (silu * pre_up).astype(BF16)

        @pl.when(core == h)
        def _():
            for sample in range(SAMPLES):
                some = hidden[sample * (rows // SAMPLES) : (sample + 1) * (rows // SAMPLES)]
                hidden_t[sample] = lax.dot_general(
                    spread, some, (((1,), (1,)), ((), ())), preferred_element_type=F32
                ).astype(BF16)

    factor_gate[...] = jnp.concatenate(gates, axis=1)
    factor_up[...] = jnp.concatenate(ups, axis=1)

    def rows_of(step):
        return pl.ds(pl.multiple_of(step * step_rows, step_rows), step_rows)

    def first(step):
        at = rows_of(step)
        wait(g_all.at[:, at], gather_sem.at[step])
        grads = jnp.concatenate([g_all[k, at, :] for k in range(chips)], axis=1)
        part_mine[at, :] = jnp.dot(grads, down_t[...], preferred_element_type=F32)
        pltpu.make_async_remote_copy(
            src_ref=part_mine.at[at],
            dst_ref=part_other.at[at],
            send_sem=part_sem.at[0, step],
            recv_sem=part_sem.at[1, step],
            device_id=sibling,
            device_id_type=MESH,
        ).start()
        pltpu.make_async_remote_copy(
            src_ref=g_all.at[:, at],
            dst_ref=g_other.at[:, at],
            send_sem=forward_sem.at[0, step],
            recv_sem=forward_sem.at[1, step],
            device_id=sibling,
            device_id_type=MESH,
        ).start()

    def second(step):
        at = rows_of(step)
        wait(part_other.at[at], part_sem.at[1, step])
        hidden_grad = part_mine[at, :] + part_other[at, :]
        both = jnp.concatenate(
            [
                (hidden_grad * factor_gate[at, :]).astype(BF16),
                (hidden_grad * factor_up[at, :]).astype(BF16),
            ],
            axis=1,
        )
        for pair in range(chips // 2):
            term = jnp.dot(
                both,
                both_t[:, :, :, pl.ds(2 * pair * CHUNK, 2 * CHUNK)].reshape(4 * units, 2 * CHUNK),
                preferred_element_type=F32,
            ).astype(BF16)
            for t in (2 * pair, 2 * pair + 1):
                send_buf[t, at, :] = term[:, (t - 2 * pair) * CHUNK : (t - 2 * pair + 1) * CHUNK]
                if t < chips - 1:
                    pltpu.make_async_remote_copy(
                        src_ref=send_buf.at[t, at],
                        dst_ref=recv_buf.at[t, at],
                        send_sem=term_sem.at[0, step],
                        recv_sem=term_sem.at[1, step],
                        device_id=(section, 2 * places[t] + core),
                        device_id_type=MESH,
                    ).start()

    def third(step):
        at = rows_of(step)
        wait(recv_buf.at[:, at], term_sem.at[1, step])
        total = send_buf[chips - 1, at, :].astype(F32)
        for t in range(chips - 1):
            total = total + recv_buf[t, at, :].astype(F32)
        result = jnp.where(is_top, top_ref[at, :], g_all[chip, at, :].astype(F32)) + total
        grad_ref[at, :] = result
        result16[at, :] = result.astype(BF16)

        @pl.when(jnp.logical_not(is_last))
        def _():
            for place in places:
                pltpu.make_async_remote_copy(
                    src_ref=result16.at[at],
                    dst_ref=g_all.at[chip, at],
                    send_sem=below_sem.at[step],
                    recv_sem=gather_sem.at[step],
                    device_id=(below, 2 * place + core),
                    device_id_type=MESH,
                ).start()

    lag = 2

    @pl.loop(0, steps)
    def _(step):
        first(step)

        @pl.when(step >= lag)
        def _():
            third(step - lag)

        second(step)

    @pl.loop(steps - lag, jnp.where(is_last, steps - lag, steps))
    def _(step):
        third(step)

    wait(w_own, load_sem.at[3])

    @pl.loop(0, steps)
    def _(step):
        wait(g_other.at[:, rows_of(step)], forward_sem.at[1, step])

    per_sample = rows // SAMPLES

    @pl.loop(0, chips // 2)
    def _(pair):
        for grads, parity in ((g_all, core), (g_other, other)):
            blocks = [2 * pair, 2 * pair + 1]
            columns = [columns_of(k, parity) for k in blocks]
            squares = None
            for sample in range(SAMPLES):
                some = jnp.concatenate(
                    [grads[k, pl.ds(sample * per_sample, per_sample), :] for k in blocks], axis=1
                )
                weight_grad = jnp.dot(hidden_t[sample], some, preferred_element_type=F32)
                square = weight_grad * weight_grad
                squares = square if squares is None else squares + square
            weight = jnp.dot(
                spread,
                jnp.concatenate([w_own[:, c] for c in columns], axis=1),
                preferred_element_type=F32,
            )
            score = jnp.abs(weight) * jnp.sqrt(squares)
            a, b, c, d = [score[i * fourth : (i + 1) * fourth] for i in range(4)]
            high_ab, low_ab = jnp.maximum(a, b), jnp.minimum(a, b)
            high_cd, low_cd = jnp.maximum(c, d), jnp.minimum(c, d)
            best = jnp.maximum(high_ab, high_cd)
            next_best = jnp.maximum(jnp.minimum(high_ab, high_cd), jnp.maximum(low_ab, low_cd))
            kept = best + next_best
            for n in range(2):
                kept_ref[:, columns[n]] = kept[:, n * CHUNK : (n + 1) * CHUNK]

    @pl.loop(jnp.where(is_last, steps - lag, steps), steps)
    def _(step):
        third(step)

    wait(both_t.at[0, core], swap_sem.at[0])
    wait(both_t.at[1, core], swap_sem.at[1])
    wait(w_down.at[core], swap_sem.at[2])
    wait(x_all.at[pl.ds(0, chips - 1)], x_sem.at[0])
    wait(pre_mine.at[0], pre_sem.at[0])
    wait(pre_mine.at[1], pre_sem.at[1])

    @pl.loop(0, steps)
    def _(step):
        at = rows_of(step)
        wait(part_mine.at[at], part_sem.at[0, step])
        wait(g_all.at[:, at], forward_sem.at[0, step])
        wait(recv_buf.at[:, at], term_sem.at[0, step])

        @pl.when(jnp.logical_not(is_last))
        def _():
            wait(g_all.at[:, at], below_sem.at[step])

        @pl.when(is_top)
        def _():
            wait(recv_buf.at[:, at], below_sem.at[steps + step])


def hand_on(grads_in, kept_in, grads_out, kept_out, sem):
    copies = [
        pltpu.make_async_copy(kept_in, kept_out, sem.at[0]),
        pltpu.make_async_copy(grads_in, grads_out, sem.at[1]),
    ]
    for copy in copies:
        copy.start()
    for copy in copies:
        copy.wait()


def shards(sections, section_inputs, top_gradient, gate_weight, up_weight, down_weight):
    _, rows, width = section_inputs.shape
    _, model, units = gate_weight.shape
    chips = model // CHUNK // 2
    step_rows = ROWS_PER_STEP
    steps = rows // step_rows
    half = chips * CHUNK
    vmem = pl.BlockSpec(memory_space=pltpu.VMEM)
    hbm = pl.BlockSpec(memory_space=pl.ANY)
    dma = pltpu.SemaphoreType.DMA
    grads, kept = pl.pallas_call(
        functools.partial(kernel, sections, chips, rows, step_rows, units),
        out_shape=(
            jax.ShapeDtypeStruct((rows, width), F32),
            jax.ShapeDtypeStruct((units // 4, model), F32),
        ),
        in_specs=[vmem, vmem, hbm, hbm, hbm],
        out_specs=(vmem, vmem),
        scratch_shapes=[
            pltpu.VMEM((2, units, half), BF16),
            pltpu.VMEM((units, model), BF16),
            pltpu.VMEM((half, 2 * units), BF16),
            pltpu.VMEM((2, 2, units, half), BF16),
            pltpu.VMEM((chips, rows, CHUNK), BF16),
            pltpu.VMEM((chips, rows, CHUNK), BF16),
            pltpu.VMEM((chips, rows, CHUNK), BF16),
            pltpu.VMEM((rows, CHUNK), BF16),
            pltpu.VMEM((rows, CHUNK), BF16),
            pltpu.VMEM((chips, rows, CHUNK), BF16),
            pltpu.VMEM((chips - 1, rows, CHUNK), BF16),
            pltpu.VMEM((rows, 2 * units), F32),
            pltpu.VMEM((rows, 2 * units), F32),
            pltpu.VMEM((2, 2, rows, units), F32),
            pltpu.VMEM((2, 2, rows, units), F32),
            pltpu.VMEM((rows, 2 * units), F32),
            pltpu.VMEM((rows, 2 * units), F32),
            pltpu.VMEM((SAMPLES, units, rows // SAMPLES), BF16),
            dma((4,)),
            dma((6,)),
            dma((2,)),
            dma((4,)),
            dma((steps,)),
            dma((2 * steps,)),
            dma((2, steps)),
            dma((2, steps)),
            dma((2, steps)),
        ],
        compiler_params=pltpu.CompilerParams(
            collective_id=0, has_side_effects=True, vmem_limit_bytes=56 * 1024 * 1024
        ),
    )(
        section_inputs[0],
        top_gradient,
        gate_weight[0].T,
        up_weight[0].T,
        down_weight[0],
    )
    grads, kept = pl.pallas_call(
        hand_on,
        out_shape=(
            jax.ShapeDtypeStruct(grads.shape, F32),
            jax.ShapeDtypeStruct(kept.shape, F32),
        ),
        in_specs=[hbm, hbm],
        out_specs=(hbm, hbm),
        scratch_shapes=[dma((2,))],
    )(grads, kept)
    return (grads[None], kept[None])


def solution(mesh):
    in_specs = (
        P("section", None, "tp"),
        P(None, "tp"),
        P("section", None, "tp"),
        P("section", None, "tp"),
        P("section", "tp", None),
    )
    out_specs = (P("section", None, "tp"), P("section", "tp", None))
    body = functools.partial(shards, mesh.shape["section"])
    return jax.shard_map(body, mesh=mesh, in_specs=in_specs, out_specs=out_specs, check_vma=False)
```

```python
import functools

import jax
import jax.numpy as jnp
from jax import lax
from jax.experimental import pallas as pl
from jax.experimental.pallas import tpu as pltpu
from jax.sharding import PartitionSpec as P

SAMPLES = 3
CHUNK = 128
ROWS_PER_STEP = 32
MESH = pl.DeviceIdType.MESH
BF16 = jnp.bfloat16
F32 = jnp.float32


def grid_sides(chips):
    side = 1
    while side * side < chips:
        side *= 2
    return chips // side, side


def ring_distance(step, size):
    return min(step, size - step)


def chip_offsets(nx, ny):
    offsets = [(dx, dy) for dx in range(nx) for dy in range(ny)]
    return sorted(offsets, key=lambda o: -(ring_distance(o[0], nx) + ring_distance(o[1], ny)))


def kernel(
    sections,
    chips,
    rows,
    step_rows,
    units,
    x_ref,
    top_ref,
    wg_hbm,
    wu_hbm,
    wd_hbm,
    grad_ref,
    kept_ref,
    w_down,
    w_own,
    down_t,
    both_t,
    x_all,
    g_all,
    g_other,
    top16,
    result16,
    send_buf,
    recv_buf,
    part_mine,
    part_other,
    pre_mine,
    pre_other,
    factor_gate,
    factor_up,
    hidden_t,
    load_sem,
    swap_sem,
    x_sem,
    pre_sem,
    gather_sem,
    below_sem,
    part_sem,
    forward_sem,
    term_sem,
):
    nx, ny = grid_sides(chips)
    offsets = chip_offsets(nx, ny)
    steps = rows // step_rows
    half = chips * CHUNK
    section = lax.axis_index("section")
    index = lax.axis_index("tp")
    chip, core = index // 2, lax.rem(index, 2)
    other = 1 - core
    chip_x, chip_y = chip // ny, lax.rem(chip, ny)
    places = [lax.rem(chip_x + dx, nx) * ny + lax.rem(chip_y + dy, ny) for dx, dy in offsets]
    sibling = (section, 2 * chip + other)
    above = lax.rem(section + 1, sections)
    below = lax.rem(section + sections - 1, sections)
    is_top = section == sections - 1
    is_last = section == 0

    def columns_of(place, parity):
        return pl.ds(pl.multiple_of((2 * place + parity) * CHUNK, CHUNK), CHUNK)

    for n, source in enumerate((wg_hbm, wu_hbm)):
        for t, place in enumerate(places):
            pltpu.make_async_copy(
                source.at[:, columns_of(place, core)],
                both_t.at[n, core, :, pl.ds(t * CHUNK, CHUNK)],
                load_sem.at[n],
            ).start()
    for k in range(chips):
        pltpu.make_async_copy(
            wd_hbm.at[:, columns_of(k, core)],
            w_down.at[core, :, pl.ds(k * CHUNK, CHUNK)],
            load_sem.at[2],
        ).start()
    pltpu.make_async_copy(wd_hbm, w_own, load_sem.at[3]).start()

    barrier = pltpu.get_barrier_semaphore()
    pl.semaphore_signal(barrier, inc=1, device_id=sibling, device_id_type=MESH)
    for place in places[:-1]:
        pl.semaphore_signal(
            barrier, inc=1, device_id=(section, 2 * place + core), device_id_type=MESH
        )

    @pl.when(jnp.logical_not(is_top))
    def _():
        for place in places:
            pl.semaphore_signal(
                barrier, inc=1, device_id=(above, 2 * place + core), device_id_type=MESH
            )

    @pl.when(jnp.logical_not(is_last))
    def _():
        for place in places:
            pl.semaphore_signal(
                barrier, inc=1, device_id=(below, 2 * place + core), device_id_type=MESH
            )

    top16[...] = top_ref[...].astype(BF16)
    neighbours = (
        chips
        + jnp.where(is_top, 0, chips)
        + jnp.where(is_last, 0, chips)
    )
    pl.semaphore_wait(barrier, neighbours)

    def spread_top(step):
        at = pl.ds(step * step_rows, step_rows)
        for place in places[:-1]:
            pltpu.make_async_remote_copy(
                src_ref=top16.at[at],
                dst_ref=g_all.at[chip, at],
                send_sem=below_sem.at[steps + step],
                recv_sem=gather_sem.at[step],
                device_id=(section, 2 * place + core),
                device_id_type=MESH,
            ).start()
        pltpu.make_async_copy(top16.at[at], g_all.at[chip, at], gather_sem.at[step]).start()

    @pl.when(is_top)
    def _():
        spread_top(0)

    for n, source in enumerate((wg_hbm, wu_hbm)):
        for t, place in enumerate(places):
            pltpu.make_async_remote_copy(
                src_ref=source.at[:, columns_of(place, other)],
                dst_ref=both_t.at[n, core, :, pl.ds(t * CHUNK, CHUNK)],
                send_sem=swap_sem.at[n],
                recv_sem=swap_sem.at[3 + n],
                device_id=sibling,
                device_id_type=MESH,
            ).start()
    for place in places[:-1]:
        pltpu.make_async_remote_copy(
            src_ref=x_ref,
            dst_ref=x_all.at[chip],
            send_sem=x_sem.at[0],
            recv_sem=x_sem.at[1],
            device_id=(section, 2 * place + core),
            device_id_type=MESH,
        ).start()
    pltpu.make_async_copy(x_ref, x_all.at[chip], x_sem.at[1]).start()
    for k in range(chips):
        pltpu.make_async_remote_copy(
            src_ref=wd_hbm.at[:, columns_of(k, other)],
            dst_ref=w_down.at[core, :, pl.ds(k * CHUNK, CHUNK)],
            send_sem=swap_sem.at[2],
            recv_sem=swap_sem.at[5],
            device_id=sibling,
            device_id_type=MESH,
        ).start()

    @pl.when(is_top)
    def _():
        for step in range(1, steps):
            spread_top(step)

    def wait(ref, sem):
        pltpu.make_async_copy(ref, ref, sem).wait()

    wait(x_all, x_sem.at[1])
    x_rows = jnp.concatenate([x_all[place] for place in places], axis=1)
    for n in range(2):
        wait(both_t.at[n, core], load_sem.at[n])
        wait(both_t.at[n, other], swap_sem.at[3 + n])
        for h in range(2):
            pre_mine[n, h] = lax.dot_general(
                x_rows, both_t[n, h], (((1,), (1,)), ((), ())), preferred_element_type=F32
            )
        pltpu.make_async_remote_copy(
            src_ref=pre_mine.at[n],
            dst_ref=pre_other.at[n],
            send_sem=pre_sem.at[n],
            recv_sem=pre_sem.at[2 + n],
            device_id=sibling,
            device_id_type=MESH,
        ).start()

    wait(w_down.at[core], load_sem.at[2])
    wait(w_down.at[other], swap_sem.at[5])
    for k in range(chips):
        at = pl.ds(k * CHUNK, CHUNK)
        down_t[at, :] = jnp.concatenate([w_down[0, :, at], w_down[1, :, at]], axis=0).T

    fourth = units // 4
    to_place = lax.broadcasted_iota(jnp.int32, (units, units), 0)
    from_unit = lax.broadcasted_iota(jnp.int32, (units, units), 1)
    member = (
        (to_place >= fourth).astype(jnp.int32)
        + (to_place >= 2 * fourth).astype(jnp.int32)
        + (to_place >= 3 * fourth).astype(jnp.int32)
    )
    spread = (from_unit == 4 * (to_place - member * fourth) + member).astype(F32).astype(BF16)

    wait(pre_other.at[0], pre_sem.at[2])
    wait(pre_other.at[1], pre_sem.at[3])
    gates, ups = [], []
    for h in range(2):
        pre_gate = pre_mine[0, h] + pre_other[0, h]
        pre_up = pre_mine[1, h] + pre_other[1, h]
        sigmoid = jax.nn.sigmoid(pre_gate)
        silu = pre_gate * sigmoid
        gates.append(pre_up * (sigmoid * (1.0 + pre_gate * (1.0 - sigmoid))))
        ups.append(silu)
        hidden = (silu * pre_up).astype(BF16)

        @pl.when(core == h)
        def _():
            for sample in range(SAMPLES):
                some = hidden[sample * (rows // SAMPLES) : (sample + 1) * (rows // SAMPLES)]
                hidden_t[sample] = lax.dot_general(
                    spread, some, (((1,), (1,)), ((), ())), preferred_element_type=F32
                ).astype(BF16)

    factor_gate[...] = jnp.concatenate(gates, axis=1)
    factor_up[...] = jnp.concatenate(ups, axis=1)

    def rows_of(step):
        return pl.ds(pl.multiple_of(step * step_rows, step_rows), step_rows)

    def first(step):
        at = rows_of(step)
        wait(g_all.at[:, at], gather_sem.at[step])
        grads = jnp.concatenate([g_all[k, at, :] for k in range(chips)], axis=1)
        part_mine[at, :] = jnp.dot(grads, down_t[...], preferred_element_type=F32)
        pltpu.make_async_remote_copy(
            src_ref=part_mine.at[at],
            dst_ref=part_other.at[at],
            send_sem=part_sem.at[0, step],
            recv_sem=part_sem.at[1, step],
            device_id=sibling,
            device_id_type=MESH,
        ).start()
        pltpu.make_async_remote_copy(
            src_ref=g_all.at[:, at],
            dst_ref=g_other.at[:, at],
            send_sem=forward_sem.at[0, step],
            recv_sem=forward_sem.at[1, step],
            device_id=sibling,
            device_id_type=MESH,
        ).start()

    def second(step):
        at = rows_of(step)
        wait(part_other.at[at], part_sem.at[1, step])
        hidden_grad = part_mine[at, :] + part_other[at, :]
        both = jnp.concatenate(
            [
                (hidden_grad * factor_gate[at, :]).astype(BF16),
                (hidden_grad * factor_up[at, :]).astype(BF16),
            ],
            axis=1,
        )
        for pair in range(chips // 2):
            term = jnp.dot(
                both,
                both_t[:, :, :, pl.ds(2 * pair * CHUNK, 2 * CHUNK)].reshape(4 * units, 2 * CHUNK),
                preferred_element_type=F32,
            ).astype(BF16)
            for t in (2 * pair, 2 * pair + 1):
                send_buf[t, at, :] = term[:, (t - 2 * pair) * CHUNK : (t - 2 * pair + 1) * CHUNK]
                if t < chips - 1:
                    pltpu.make_async_remote_copy(
                        src_ref=send_buf.at[t, at],
                        dst_ref=recv_buf.at[t, at],
                        send_sem=term_sem.at[0, step],
                        recv_sem=term_sem.at[1, step],
                        device_id=(section, 2 * places[t] + core),
                        device_id_type=MESH,
                    ).start()

    def third(step):
        at = rows_of(step)
        wait(recv_buf.at[:, at], term_sem.at[1, step])
        total = send_buf[chips - 1, at, :].astype(F32)
        for t in range(chips - 1):
            total = total + recv_buf[t, at, :].astype(F32)
        result = jnp.where(is_top, top_ref[at, :], g_all[chip, at, :].astype(F32)) + total
        grad_ref[at, :] = result
        result16[at, :] = result.astype(BF16)

        @pl.when(jnp.logical_not(is_last))
        def _():
            for place in places:
                pltpu.make_async_remote_copy(
                    src_ref=result16.at[at],
                    dst_ref=g_all.at[chip, at],
                    send_sem=below_sem.at[step],
                    recv_sem=gather_sem.at[step],
                    device_id=(below, 2 * place + core),
                    device_id_type=MESH,
                ).start()

    lag = 2

    @pl.loop(0, steps)
    def _(step):
        @pl.when(step >= lag)
        def _():
            third(step - lag)

        first(step)
        second(step)

    @pl.loop(steps - lag, jnp.where(is_last, steps - lag, steps))
    def _(step):
        third(step)

    wait(w_own, load_sem.at[3])

    @pl.loop(0, steps)
    def _(step):
        wait(g_other.at[:, rows_of(step)], forward_sem.at[1, step])

    per_sample = rows // SAMPLES

    @pl.loop(0, chips // 2)
    def _(pair):
        for grads, parity in ((g_all, core), (g_other, other)):
            blocks = [2 * pair, 2 * pair + 1]
            columns = [columns_of(k, parity) for k in blocks]
            squares = None
            for sample in range(SAMPLES):
                some = jnp.concatenate(
                    [grads[k, pl.ds(sample * per_sample, per_sample), :] for k in blocks], axis=1
                )
                weight_grad = jnp.dot(hidden_t[sample], some, preferred_element_type=F32)
                square = weight_grad * weight_grad
                squares = square if squares is None else squares + square
            weight = jnp.dot(
                spread,
                jnp.concatenate([w_own[:, c] for c in columns], axis=1),
                preferred_element_type=F32,
            )
            score = jnp.abs(weight) * jnp.sqrt(squares)
            a, b, c, d = [score[i * fourth : (i + 1) * fourth] for i in range(4)]
            high_ab, low_ab = jnp.maximum(a, b), jnp.minimum(a, b)
            high_cd, low_cd = jnp.maximum(c, d), jnp.minimum(c, d)
            best = jnp.maximum(high_ab, high_cd)
            next_best = jnp.maximum(jnp.minimum(high_ab, high_cd), jnp.maximum(low_ab, low_cd))
            kept = best + next_best
            for n in range(2):
                kept_ref[:, columns[n]] = kept[:, n * CHUNK : (n + 1) * CHUNK]

    @pl.loop(jnp.where(is_last, steps - lag, steps), steps)
    def _(step):
        third(step)

    wait(both_t.at[0, core], swap_sem.at[0])
    wait(both_t.at[1, core], swap_sem.at[1])
    wait(w_down.at[core], swap_sem.at[2])
    wait(x_all.at[pl.ds(0, chips - 1)], x_sem.at[0])
    wait(pre_mine.at[0], pre_sem.at[0])
    wait(pre_mine.at[1], pre_sem.at[1])

    @pl.loop(0, steps)
    def _(step):
        at = rows_of(step)
        wait(part_mine.at[at], part_sem.at[0, step])
        wait(g_all.at[:, at], forward_sem.at[0, step])
        wait(recv_buf.at[:, at], term_sem.at[0, step])

        @pl.when(jnp.logical_not(is_last))
        def _():
            wait(g_all.at[:, at], below_sem.at[step])

        @pl.when(is_top)
        def _():
            wait(recv_buf.at[:, at], below_sem.at[steps + step])


def hand_on(grads_in, kept_in, grads_out, kept_out):
    grads_out[...] = grads_in[...]
    kept_out[...] = kept_in[...]


def shards(sections, section_inputs, top_gradient, gate_weight, up_weight, down_weight):
    _, rows, width = section_inputs.shape
    _, model, units = gate_weight.shape
    chips = model // CHUNK // 2
    step_rows = ROWS_PER_STEP
    steps = rows // step_rows
    half = chips * CHUNK
    vmem = pl.BlockSpec(memory_space=pltpu.VMEM)
    hbm = pl.BlockSpec(memory_space=pl.ANY)
    dma = pltpu.SemaphoreType.DMA
    grads, kept = pl.pallas_call(
        functools.partial(kernel, sections, chips, rows, step_rows, units),
        out_shape=(
            jax.ShapeDtypeStruct((rows, width), F32),
            jax.ShapeDtypeStruct((units // 4, model), F32),
        ),
        in_specs=[vmem, vmem, hbm, hbm, hbm],
        out_specs=(vmem, vmem),
        scratch_shapes=[
            pltpu.VMEM((2, units, half), BF16),
            pltpu.VMEM((units, model), BF16),
            pltpu.VMEM((half, 2 * units), BF16),
            pltpu.VMEM((2, 2, units, half), BF16),
            pltpu.VMEM((chips, rows, CHUNK), BF16),
            pltpu.VMEM((chips, rows, CHUNK), BF16),
            pltpu.VMEM((chips, rows, CHUNK), BF16),
            pltpu.VMEM((rows, CHUNK), BF16),
            pltpu.VMEM((rows, CHUNK), BF16),
            pltpu.VMEM((chips, rows, CHUNK), BF16),
            pltpu.VMEM((chips - 1, rows, CHUNK), BF16),
            pltpu.VMEM((rows, 2 * units), F32),
            pltpu.VMEM((rows, 2 * units), F32),
            pltpu.VMEM((2, 2, rows, units), F32),
            pltpu.VMEM((2, 2, rows, units), F32),
            pltpu.VMEM((rows, 2 * units), F32),
            pltpu.VMEM((rows, 2 * units), F32),
            pltpu.VMEM((SAMPLES, units, rows // SAMPLES), BF16),
            dma((4,)),
            dma((6,)),
            dma((2,)),
            dma((4,)),
            dma((steps,)),
            dma((2 * steps,)),
            dma((2, steps)),
            dma((2, steps)),
            dma((2, steps)),
        ],
        compiler_params=pltpu.CompilerParams(
            collective_id=0, has_side_effects=True, vmem_limit_bytes=56 * 1024 * 1024
        ),
    )(
        section_inputs[0],
        top_gradient,
        gate_weight[0].T,
        up_weight[0].T,
        down_weight[0],
    )
    grads, kept = pl.pallas_call(
        hand_on,
        out_shape=(
            jax.ShapeDtypeStruct(grads.shape, F32),
            jax.ShapeDtypeStruct(kept.shape, F32),
        ),
        in_specs=[vmem, vmem],
        out_specs=(vmem, vmem),
    )(grads, kept)
    return (grads[None], kept[None])


def solution(mesh):
    in_specs = (
        P("section", None, "tp"),
        P(None, "tp"),
        P("section", None, "tp"),
        P("section", None, "tp"),
        P("section", "tp", None),
    )
    out_specs = (P("section", None, "tp"), P("section", "tp", None))
    body = functools.partial(shards, mesh.shape["section"])
    return jax.shard_map(body, mesh=mesh, in_specs=in_specs, out_specs=out_specs, check_vma=False)
```

```python
import functools

import jax
import jax.numpy as jnp
from jax import lax
from jax.experimental import pallas as pl
from jax.experimental.pallas import tpu as pltpu
from jax.sharding import PartitionSpec as P

SAMPLES = 3
CHUNK = 128
ROWS_PER_STEP = 32
MESH = pl.DeviceIdType.MESH
BF16 = jnp.bfloat16
F32 = jnp.float32


def grid_sides(chips):
    side = 1
    while side * side < chips:
        side *= 2
    return chips // side, side


def ring_distance(step, size):
    return min(step, size - step)


def chip_offsets(nx, ny):
    offsets = [(dx, dy) for dx in range(nx) for dy in range(ny)]
    return sorted(offsets, key=lambda o: -(ring_distance(o[0], nx) + ring_distance(o[1], ny)))


def kernel(
    sections,
    chips,
    rows,
    step_rows,
    units,
    x_ref,
    top_ref,
    wg_hbm,
    wu_hbm,
    wd_hbm,
    grad_ref,
    kept_ref,
    w_down,
    w_own,
    down_t,
    both_t,
    x_all,
    g_all,
    g_other,
    top16,
    result16,
    send_buf,
    recv_buf,
    part_mine,
    part_other,
    pre_mine,
    pre_other,
    factor_gate,
    factor_up,
    hidden_t,
    load_sem,
    swap_sem,
    x_sem,
    pre_sem,
    gather_sem,
    below_sem,
    part_sem,
    forward_sem,
    term_sem,
):
    nx, ny = grid_sides(chips)
    offsets = chip_offsets(nx, ny)
    steps = rows // step_rows
    half = chips * CHUNK
    section = lax.axis_index("section")
    index = lax.axis_index("tp")
    chip, core = index // 2, lax.rem(index, 2)
    other = 1 - core
    chip_x, chip_y = chip // ny, lax.rem(chip, ny)
    places = [lax.rem(chip_x + dx, nx) * ny + lax.rem(chip_y + dy, ny) for dx, dy in offsets]
    sibling = (section, 2 * chip + other)
    above = lax.rem(section + 1, sections)
    below = lax.rem(section + sections - 1, sections)
    is_top = section == sections - 1
    is_last = section == 0

    def columns_of(place, parity):
        return pl.ds(pl.multiple_of((2 * place + parity) * CHUNK, CHUNK), CHUNK)

    for n, source in enumerate((wg_hbm, wu_hbm)):
        for t, place in enumerate(places):
            pltpu.make_async_copy(
                source.at[:, columns_of(place, core)],
                both_t.at[n, core, :, pl.ds(t * CHUNK, CHUNK)],
                load_sem.at[n],
            ).start()
    for k in range(chips):
        pltpu.make_async_copy(
            wd_hbm.at[:, columns_of(k, core)],
            w_down.at[core, :, pl.ds(k * CHUNK, CHUNK)],
            load_sem.at[2],
        ).start()
    pltpu.make_async_copy(wd_hbm, w_own, load_sem.at[3]).start()

    barrier = pltpu.get_barrier_semaphore()
    pl.semaphore_signal(barrier, inc=1, device_id=sibling, device_id_type=MESH)
    for place in places[:-1]:
        pl.semaphore_signal(
            barrier, inc=1, device_id=(section, 2 * place + core), device_id_type=MESH
        )

    @pl.when(jnp.logical_not(is_top))
    def _():
        for place in places:
            pl.semaphore_signal(
                barrier, inc=1, device_id=(above, 2 * place + core), device_id_type=MESH
            )

    @pl.when(jnp.logical_not(is_last))
    def _():
        for place in places:
            pl.semaphore_signal(
                barrier, inc=1, device_id=(below, 2 * place + core), device_id_type=MESH
            )

    top16[...] = top_ref[...].astype(BF16)
    neighbours = (
        chips
        + jnp.where(is_top, 0, chips)
        + jnp.where(is_last, 0, chips)
    )
    pl.semaphore_wait(barrier, neighbours)

    def spread_top(step):
        at = pl.ds(step * step_rows, step_rows)
        for place in places[:-1]:
            pltpu.make_async_remote_copy(
                src_ref=top16.at[at],
                dst_ref=g_all.at[chip, at],
                send_sem=below_sem.at[steps + step],
                recv_sem=gather_sem.at[step],
                device_id=(section, 2 * place + core),
                device_id_type=MESH,
            ).start()
        pltpu.make_async_copy(top16.at[at], g_all.at[chip, at], gather_sem.at[step]).start()

    for place in places[:-1]:
        pltpu.make_async_remote_copy(
            src_ref=x_ref,
            dst_ref=x_all.at[chip],
            send_sem=x_sem.at[0],
            recv_sem=x_sem.at[1],
            device_id=(section, 2 * place + core),
            device_id_type=MESH,
        ).start()
    pltpu.make_async_copy(x_ref, x_all.at[chip], x_sem.at[1]).start()
    @pl.when(is_top)
    def _():
        spread_top(0)

    for n, source in enumerate((wg_hbm, wu_hbm)):
        for t, place in enumerate(places):
            pltpu.make_async_remote_copy(
                src_ref=source.at[:, columns_of(place, other)],
                dst_ref=both_t.at[n, core, :, pl.ds(t * CHUNK, CHUNK)],
                send_sem=swap_sem.at[n],
                recv_sem=swap_sem.at[3 + n],
                device_id=sibling,
                device_id_type=MESH,
            ).start()
    for k in range(chips):
        pltpu.make_async_remote_copy(
            src_ref=wd_hbm.at[:, columns_of(k, other)],
            dst_ref=w_down.at[core, :, pl.ds(k * CHUNK, CHUNK)],
            send_sem=swap_sem.at[2],
            recv_sem=swap_sem.at[5],
            device_id=sibling,
            device_id_type=MESH,
        ).start()

    @pl.when(is_top)
    def _():
        for step in range(1, steps):
            spread_top(step)

    def wait(ref, sem):
        pltpu.make_async_copy(ref, ref, sem).wait()

    wait(x_all, x_sem.at[1])
    x_rows = jnp.concatenate([x_all[place] for place in places], axis=1)
    for n in range(2):
        wait(both_t.at[n, core], load_sem.at[n])
        wait(both_t.at[n, other], swap_sem.at[3 + n])
        for h in range(2):
            pre_mine[n, h] = lax.dot_general(
                x_rows, both_t[n, h], (((1,), (1,)), ((), ())), preferred_element_type=F32
            )
        pltpu.make_async_remote_copy(
            src_ref=pre_mine.at[n],
            dst_ref=pre_other.at[n],
            send_sem=pre_sem.at[n],
            recv_sem=pre_sem.at[2 + n],
            device_id=sibling,
            device_id_type=MESH,
        ).start()

    wait(w_down.at[core], load_sem.at[2])
    wait(w_down.at[other], swap_sem.at[5])
    for k in range(chips):
        at = pl.ds(k * CHUNK, CHUNK)
        down_t[at, :] = jnp.concatenate([w_down[0, :, at], w_down[1, :, at]], axis=0).T

    fourth = units // 4
    to_place = lax.broadcasted_iota(jnp.int32, (units, units), 0)
    from_unit = lax.broadcasted_iota(jnp.int32, (units, units), 1)
    member = (
        (to_place >= fourth).astype(jnp.int32)
        + (to_place >= 2 * fourth).astype(jnp.int32)
        + (to_place >= 3 * fourth).astype(jnp.int32)
    )
    spread = (from_unit == 4 * (to_place - member * fourth) + member).astype(F32).astype(BF16)

    wait(pre_other.at[0], pre_sem.at[2])
    wait(pre_other.at[1], pre_sem.at[3])
    gates, ups = [], []
    for h in range(2):
        pre_gate = pre_mine[0, h] + pre_other[0, h]
        pre_up = pre_mine[1, h] + pre_other[1, h]
        sigmoid = jax.nn.sigmoid(pre_gate)
        silu = pre_gate * sigmoid
        gates.append(pre_up * (sigmoid * (1.0 + pre_gate * (1.0 - sigmoid))))
        ups.append(silu)
        hidden = (silu * pre_up).astype(BF16)

        @pl.when(core == h)
        def _():
            for sample in range(SAMPLES):
                some = hidden[sample * (rows // SAMPLES) : (sample + 1) * (rows // SAMPLES)]
                hidden_t[sample] = lax.dot_general(
                    spread, some, (((1,), (1,)), ((), ())), preferred_element_type=F32
                ).astype(BF16)

    factor_gate[...] = jnp.concatenate(gates, axis=1)
    factor_up[...] = jnp.concatenate(ups, axis=1)

    def rows_of(step):
        return pl.ds(pl.multiple_of(step * step_rows, step_rows), step_rows)

    def first(step):
        at = rows_of(step)
        wait(g_all.at[:, at], gather_sem.at[step])
        grads = jnp.concatenate([g_all[k, at, :] for k in range(chips)], axis=1)
        part_mine[at, :] = jnp.dot(grads, down_t[...], preferred_element_type=F32)
        pltpu.make_async_remote_copy(
            src_ref=part_mine.at[at],
            dst_ref=part_other.at[at],
            send_sem=part_sem.at[0, step],
            recv_sem=part_sem.at[1, step],
            device_id=sibling,
            device_id_type=MESH,
        ).start()
        pltpu.make_async_remote_copy(
            src_ref=g_all.at[:, at],
            dst_ref=g_other.at[:, at],
            send_sem=forward_sem.at[0, step],
            recv_sem=forward_sem.at[1, step],
            device_id=sibling,
            device_id_type=MESH,
        ).start()

    def second(step):
        at = rows_of(step)
        wait(part_other.at[at], part_sem.at[1, step])
        hidden_grad = part_mine[at, :] + part_other[at, :]
        both = jnp.concatenate(
            [
                (hidden_grad * factor_gate[at, :]).astype(BF16),
                (hidden_grad * factor_up[at, :]).astype(BF16),
            ],
            axis=1,
        )
        for four in range(chips // 4):
            term = jnp.dot(
                both,
                both_t[:, :, :, pl.ds(4 * four * CHUNK, 4 * CHUNK)].reshape(4 * units, 4 * CHUNK),
                preferred_element_type=F32,
            ).astype(BF16)
            for t in range(4 * four, 4 * four + 4):
                send_buf[t, at, :] = term[:, (t - 4 * four) * CHUNK : (t - 4 * four + 1) * CHUNK]
                if t < chips - 1:
                    pltpu.make_async_remote_copy(
                        src_ref=send_buf.at[t, at],
                        dst_ref=recv_buf.at[t, at],
                        send_sem=term_sem.at[0, step],
                        recv_sem=term_sem.at[1, step],
                        device_id=(section, 2 * places[t] + core),
                        device_id_type=MESH,
                    ).start()

    def third(step):
        at = rows_of(step)
        wait(recv_buf.at[:, at], term_sem.at[1, step])
        total = send_buf[chips - 1, at, :].astype(F32)
        for t in range(chips - 1):
            total = total + recv_buf[t, at, :].astype(F32)
        result = jnp.where(is_top, top_ref[at, :], g_all[chip, at, :].astype(F32)) + total
        grad_ref[at, :] = result
        result16[at, :] = result.astype(BF16)

        @pl.when(jnp.logical_not(is_last))
        def _():
            for place in places:
                pltpu.make_async_remote_copy(
                    src_ref=result16.at[at],
                    dst_ref=g_all.at[chip, at],
                    send_sem=below_sem.at[step],
                    recv_sem=gather_sem.at[step],
                    device_id=(below, 2 * place + core),
                    device_id_type=MESH,
                ).start()

    lag = 2

    @pl.loop(0, steps)
    def _(step):
        first(step)

        @pl.when(step >= lag)
        def _():
            third(step - lag)

        second(step)

    @pl.loop(steps - lag, jnp.where(is_last, steps - lag, steps))
    def _(step):
        third(step)

    wait(w_own, load_sem.at[3])

    @pl.loop(0, steps)
    def _(step):
        wait(g_other.at[:, rows_of(step)], forward_sem.at[1, step])

    per_sample = rows // SAMPLES

    @pl.loop(0, chips // 2)
    def _(pair):
        for grads, parity in ((g_all, core), (g_other, other)):
            blocks = [2 * pair, 2 * pair + 1]
            columns = [columns_of(k, parity) for k in blocks]
            squares = None
            for sample in range(SAMPLES):
                some = jnp.concatenate(
                    [grads[k, pl.ds(sample * per_sample, per_sample), :] for k in blocks], axis=1
                )
                weight_grad = jnp.dot(hidden_t[sample], some, preferred_element_type=F32)
                square = weight_grad * weight_grad
                squares = square if squares is None else squares + square
            weight = jnp.dot(
                spread,
                jnp.concatenate([w_own[:, c] for c in columns], axis=1),
                preferred_element_type=F32,
            )
            score = jnp.abs(weight) * jnp.sqrt(squares)
            a, b, c, d = [score[i * fourth : (i + 1) * fourth] for i in range(4)]
            high_ab, low_ab = jnp.maximum(a, b), jnp.minimum(a, b)
            high_cd, low_cd = jnp.maximum(c, d), jnp.minimum(c, d)
            best = jnp.maximum(high_ab, high_cd)
            next_best = jnp.maximum(jnp.minimum(high_ab, high_cd), jnp.maximum(low_ab, low_cd))
            kept = best + next_best
            for n in range(2):
                kept_ref[:, columns[n]] = kept[:, n * CHUNK : (n + 1) * CHUNK]

    @pl.loop(jnp.where(is_last, steps - lag, steps), steps)
    def _(step):
        third(step)

    wait(both_t.at[0, core], swap_sem.at[0])
    wait(both_t.at[1, core], swap_sem.at[1])
    wait(w_down.at[core], swap_sem.at[2])
    wait(x_all.at[pl.ds(0, chips - 1)], x_sem.at[0])
    wait(pre_mine.at[0], pre_sem.at[0])
    wait(pre_mine.at[1], pre_sem.at[1])

    @pl.loop(0, steps)
    def _(step):
        at = rows_of(step)
        wait(part_mine.at[at], part_sem.at[0, step])
        wait(g_all.at[:, at], forward_sem.at[0, step])
        wait(recv_buf.at[:, at], term_sem.at[0, step])

        @pl.when(jnp.logical_not(is_last))
        def _():
            wait(g_all.at[:, at], below_sem.at[step])

        @pl.when(is_top)
        def _():
            wait(recv_buf.at[:, at], below_sem.at[steps + step])


def hand_on(grads_in, kept_in, grads_out, kept_out):
    grads_out[...] = grads_in[...]
    kept_out[...] = kept_in[...]


def shards(sections, section_inputs, top_gradient, gate_weight, up_weight, down_weight):
    _, rows, width = section_inputs.shape
    _, model, units = gate_weight.shape
    chips = model // CHUNK // 2
    step_rows = ROWS_PER_STEP
    steps = rows // step_rows
    half = chips * CHUNK
    vmem = pl.BlockSpec(memory_space=pltpu.VMEM)
    hbm = pl.BlockSpec(memory_space=pl.ANY)
    dma = pltpu.SemaphoreType.DMA
    grads, kept = pl.pallas_call(
        functools.partial(kernel, sections, chips, rows, step_rows, units),
        out_shape=(
            jax.ShapeDtypeStruct((rows, width), F32),
            jax.ShapeDtypeStruct((units // 4, model), F32),
        ),
        in_specs=[vmem, vmem, hbm, hbm, hbm],
        out_specs=(vmem, vmem),
        scratch_shapes=[
            pltpu.VMEM((2, units, half), BF16),
            pltpu.VMEM((units, model), BF16),
            pltpu.VMEM((half, 2 * units), BF16),
            pltpu.VMEM((2, 2, units, half), BF16),
            pltpu.VMEM((chips, rows, CHUNK), BF16),
            pltpu.VMEM((chips, rows, CHUNK), BF16),
            pltpu.VMEM((chips, rows, CHUNK), BF16),
            pltpu.VMEM((rows, CHUNK), BF16),
            pltpu.VMEM((rows, CHUNK), BF16),
            pltpu.VMEM((chips, rows, CHUNK), BF16),
            pltpu.VMEM((chips - 1, rows, CHUNK), BF16),
            pltpu.VMEM((rows, 2 * units), F32),
            pltpu.VMEM((rows, 2 * units), F32),
            pltpu.VMEM((2, 2, rows, units), F32),
            pltpu.VMEM((2, 2, rows, units), F32),
            pltpu.VMEM((rows, 2 * units), F32),
            pltpu.VMEM((rows, 2 * units), F32),
            pltpu.VMEM((SAMPLES, units, rows // SAMPLES), BF16),
            dma((4,)),
            dma((6,)),
            dma((2,)),
            dma((4,)),
            dma((steps,)),
            dma((2 * steps,)),
            dma((2, steps)),
            dma((2, steps)),
            dma((2, steps)),
        ],
        compiler_params=pltpu.CompilerParams(
            collective_id=0, has_side_effects=True, vmem_limit_bytes=56 * 1024 * 1024
        ),
    )(
        section_inputs[0],
        top_gradient,
        gate_weight[0].T,
        up_weight[0].T,
        down_weight[0],
    )
    grads, kept = pl.pallas_call(
        hand_on,
        out_shape=(
            jax.ShapeDtypeStruct(grads.shape, F32),
            jax.ShapeDtypeStruct(kept.shape, F32),
        ),
        in_specs=[vmem, vmem],
        out_specs=(vmem, vmem),
    )(grads, kept)
    return (grads[None], kept[None])


def solution(mesh):
    in_specs = (
        P("section", None, "tp"),
        P(None, "tp"),
        P("section", None, "tp"),
        P("section", None, "tp"),
        P("section", "tp", None),
    )
    out_specs = (P("section", None, "tp"), P("section", "tp", None))
    body = functools.partial(shards, mesh.shape["section"])
    return jax.shard_map(body, mesh=mesh, in_specs=in_specs, out_specs=out_specs, check_vma=False)
```

```python
import functools

import jax
import jax.numpy as jnp
from jax import lax
from jax.experimental import pallas as pl
from jax.experimental.pallas import tpu as pltpu
from jax.sharding import PartitionSpec as P

SAMPLES = 3
CHUNK = 128
ROWS_PER_STEP = 32
MESH = pl.DeviceIdType.MESH
BF16 = jnp.bfloat16
F32 = jnp.float32


def grid_sides(chips):
    side = 1
    while side * side < chips:
        side *= 2
    return chips // side, side


def ring_distance(step, size):
    return min(step, size - step)


def chip_offsets(nx, ny):
    offsets = [(dx, dy) for dx in range(nx) for dy in range(ny)]
    return sorted(offsets, key=lambda o: -(ring_distance(o[0], nx) + ring_distance(o[1], ny)))


def kernel(
    sections,
    chips,
    rows,
    step_rows,
    units,
    x_ref,
    top_ref,
    wg_hbm,
    wu_hbm,
    wd_hbm,
    grad_ref,
    kept_ref,
    w_down,
    w_own,
    down_t,
    both_t,
    x_all,
    g_all,
    g_other,
    top16,
    result16,
    send_buf,
    recv_buf,
    part_mine,
    part_send,
    part_other,
    pre_mine,
    pre_send,
    pre_other,
    factor_gate,
    factor_up,
    hidden_t,
    load_sem,
    swap_sem,
    x_sem,
    pre_sem,
    gather_sem,
    below_sem,
    part_sem,
    forward_sem,
    term_sem,
):
    nx, ny = grid_sides(chips)
    offsets = chip_offsets(nx, ny)
    steps = rows // step_rows
    half = chips * CHUNK
    section = lax.axis_index("section")
    index = lax.axis_index("tp")
    chip, core = index // 2, lax.rem(index, 2)
    other = 1 - core
    chip_x, chip_y = chip // ny, lax.rem(chip, ny)
    places = [lax.rem(chip_x + dx, nx) * ny + lax.rem(chip_y + dy, ny) for dx, dy in offsets]
    sibling = (section, 2 * chip + other)
    above = lax.rem(section + 1, sections)
    below = lax.rem(section + sections - 1, sections)
    is_top = section == sections - 1
    is_last = section == 0

    def columns_of(place, parity):
        return pl.ds(pl.multiple_of((2 * place + parity) * CHUNK, CHUNK), CHUNK)

    for n, source in enumerate((wg_hbm, wu_hbm)):
        for t, place in enumerate(places):
            pltpu.make_async_copy(
                source.at[:, columns_of(place, core)],
                both_t.at[n, core, :, pl.ds(t * CHUNK, CHUNK)],
                load_sem.at[n],
            ).start()
    for k in range(chips):
        pltpu.make_async_copy(
            wd_hbm.at[:, columns_of(k, core)],
            w_down.at[core, :, pl.ds(k * CHUNK, CHUNK)],
            load_sem.at[2],
        ).start()
    pltpu.make_async_copy(wd_hbm, w_own, load_sem.at[3]).start()

    barrier = pltpu.get_barrier_semaphore()
    pl.semaphore_signal(barrier, inc=1, device_id=sibling, device_id_type=MESH)
    for place in places[:-1]:
        pl.semaphore_signal(
            barrier, inc=1, device_id=(section, 2 * place + core), device_id_type=MESH
        )

    @pl.when(jnp.logical_not(is_top))
    def _():
        for place in places:
            pl.semaphore_signal(
                barrier, inc=1, device_id=(above, 2 * place + core), device_id_type=MESH
            )

    @pl.when(jnp.logical_not(is_last))
    def _():
        for place in places:
            pl.semaphore_signal(
                barrier, inc=1, device_id=(below, 2 * place + core), device_id_type=MESH
            )

    top16[...] = top_ref[...].astype(BF16)
    neighbours = (
        chips
        + jnp.where(is_top, 0, chips)
        + jnp.where(is_last, 0, chips)
    )
    pl.semaphore_wait(barrier, neighbours)

    def spread_top(step):
        at = pl.ds(step * step_rows, step_rows)
        for place in places[:-1]:
            pltpu.make_async_remote_copy(
                src_ref=top16.at[at],
                dst_ref=g_all.at[chip, at],
                send_sem=below_sem.at[steps + step],
                recv_sem=gather_sem.at[step],
                device_id=(section, 2 * place + core),
                device_id_type=MESH,
            ).start()
        pltpu.make_async_copy(top16.at[at], g_all.at[chip, at], gather_sem.at[step]).start()

    first_rows = rows // SAMPLES
    parts = (pl.ds(0, first_rows), pl.ds(first_rows, rows - first_rows))

    def spread_x(part):
        at = parts[part]
        for place in places[:-1]:
            pltpu.make_async_remote_copy(
                src_ref=x_ref.at[at],
                dst_ref=x_all.at[chip, at],
                send_sem=x_sem.at[part],
                recv_sem=x_sem.at[2 + part],
                device_id=(section, 2 * place + core),
                device_id_type=MESH,
            ).start()
        pltpu.make_async_copy(x_ref.at[at], x_all.at[chip, at], x_sem.at[2 + part]).start()

    spread_x(0)

    @pl.when(is_top)
    def _():
        spread_top(0)
        spread_top(1)

    spread_x(1)

    for n, source in enumerate((wg_hbm, wu_hbm)):
        for t, place in enumerate(places):
            pltpu.make_async_remote_copy(
                src_ref=source.at[:, columns_of(place, other)],
                dst_ref=both_t.at[n, core, :, pl.ds(t * CHUNK, CHUNK)],
                send_sem=swap_sem.at[n],
                recv_sem=swap_sem.at[3 + n],
                device_id=sibling,
                device_id_type=MESH,
            ).start()
    for k in range(chips):
        pltpu.make_async_remote_copy(
            src_ref=wd_hbm.at[:, columns_of(k, other)],
            dst_ref=w_down.at[core, :, pl.ds(k * CHUNK, CHUNK)],
            send_sem=swap_sem.at[2],
            recv_sem=swap_sem.at[5],
            device_id=sibling,
            device_id_type=MESH,
        ).start()

    @pl.when(is_top)
    def _():
        for step in range(2, steps):
            spread_top(step)

    def wait(ref, sem):
        pltpu.make_async_copy(ref, ref, sem).wait()

    def forward_start(part):
        at = parts[part]
        wait(x_all.at[:, at], x_sem.at[2 + part])
        x_rows = jnp.concatenate([x_all[place, at, :] for place in places], axis=1)
        for n in range(2):
            if part == 0:
                wait(both_t.at[n, core], load_sem.at[n])
                wait(both_t.at[n, other], swap_sem.at[3 + n])
            for h in range(2):
                partial = lax.dot_general(
                    x_rows, both_t[n, h], (((1,), (1,)), ((), ())), preferred_element_type=F32
                )
                pre_mine[n, h, at, :] = partial
                pre_send[n, h, at, :] = partial.astype(BF16)
                pltpu.make_async_remote_copy(
                    src_ref=pre_send.at[n, h, at],
                    dst_ref=pre_other.at[n, h, at],
                    send_sem=pre_sem.at[0, part, 2 * n + h],
                    recv_sem=pre_sem.at[1, part, 2 * n + h],
                    device_id=sibling,
                    device_id_type=MESH,
                ).start()

    forward_start(0)

    @pl.when(jnp.logical_not(is_top))
    def _():
        forward_start(1)

    wait(w_down.at[core], load_sem.at[2])
    wait(w_down.at[other], swap_sem.at[5])
    for k in range(chips):
        at = pl.ds(k * CHUNK, CHUNK)
        down_t[at, :] = jnp.concatenate([w_down[0, :, at], w_down[1, :, at]], axis=0).T

    fourth = units // 4
    to_place = lax.broadcasted_iota(jnp.int32, (units, units), 0)
    from_unit = lax.broadcasted_iota(jnp.int32, (units, units), 1)
    member = (
        (to_place >= fourth).astype(jnp.int32)
        + (to_place >= 2 * fourth).astype(jnp.int32)
        + (to_place >= 3 * fourth).astype(jnp.int32)
    )
    spread = (from_unit == 4 * (to_place - member * fourth) + member).astype(F32).astype(BF16)

    def rows_of(step):
        return pl.ds(pl.multiple_of(step * step_rows, step_rows), step_rows)

    def first(step):
        at = rows_of(step)
        wait(g_all.at[:, at], gather_sem.at[step])
        grads = jnp.concatenate([g_all[k, at, :] for k in range(chips)], axis=1)
        partial = jnp.dot(grads, down_t[...], preferred_element_type=F32)
        part_mine[at, :] = partial
        part_send[at, :] = partial.astype(BF16)
        pltpu.make_async_remote_copy(
            src_ref=part_send.at[at],
            dst_ref=part_other.at[at],
            send_sem=part_sem.at[0, step],
            recv_sem=part_sem.at[1, step],
            device_id=sibling,
            device_id_type=MESH,
        ).start()
        pltpu.make_async_remote_copy(
            src_ref=g_all.at[:, at],
            dst_ref=g_other.at[:, at],
            send_sem=forward_sem.at[0, step],
            recv_sem=forward_sem.at[1, step],
            device_id=sibling,
            device_id_type=MESH,
        ).start()

    def second(step):
        at = rows_of(step)
        wait(part_other.at[at], part_sem.at[1, step])
        hidden_grad = part_mine[at, :] + part_other[at, :].astype(F32)
        both = jnp.concatenate(
            [
                (hidden_grad * factor_gate[at, :]).astype(BF16),
                (hidden_grad * factor_up[at, :]).astype(BF16),
            ],
            axis=1,
        )
        for four in range(chips // 4):
            term = jnp.dot(
                both,
                both_t[:, :, :, pl.ds(4 * four * CHUNK, 4 * CHUNK)].reshape(4 * units, 4 * CHUNK),
                preferred_element_type=F32,
            ).astype(BF16)
            for t in range(4 * four, 4 * four + 4):
                send_buf[t, at, :] = term[:, (t - 4 * four) * CHUNK : (t - 4 * four + 1) * CHUNK]
                if t < chips - 1:
                    pltpu.make_async_remote_copy(
                        src_ref=send_buf.at[t, at],
                        dst_ref=recv_buf.at[t, at],
                        send_sem=term_sem.at[0, step],
                        recv_sem=term_sem.at[1, step],
                        device_id=(section, 2 * places[t] + core),
                        device_id_type=MESH,
                    ).start()

    def third(step):
        at = rows_of(step)
        wait(recv_buf.at[:, at], term_sem.at[1, step])
        total = send_buf[chips - 1, at, :].astype(F32)
        for t in range(chips - 1):
            total = total + recv_buf[t, at, :].astype(F32)
        result = jnp.where(is_top, top_ref[at, :], g_all[chip, at, :].astype(F32)) + total
        grad_ref[at, :] = result
        result16[at, :] = result.astype(BF16)

        @pl.when(jnp.logical_not(is_last))
        def _():
            for place in places:
                pltpu.make_async_remote_copy(
                    src_ref=result16.at[at],
                    dst_ref=g_all.at[chip, at],
                    send_sem=below_sem.at[step],
                    recv_sem=gather_sem.at[step],
                    device_id=(below, 2 * place + core),
                    device_id_type=MESH,
                ).start()

    @pl.when(is_top)
    def _():
        first(0)

    def forward_end(part):
        at = parts[part]
        gates, ups = [], []
        for h in range(2):
            wait(pre_other.at[0, h, at], pre_sem.at[1, part, h])
            wait(pre_other.at[1, h, at], pre_sem.at[1, part, 2 + h])
            pre_gate = pre_mine[0, h, at, :] + pre_other[0, h, at, :].astype(F32)
            pre_up = pre_mine[1, h, at, :] + pre_other[1, h, at, :].astype(F32)
            sigmoid = jax.nn.sigmoid(pre_gate)
            silu = pre_gate * sigmoid
            gates.append(pre_up * (sigmoid * (1.0 + pre_gate * (1.0 - sigmoid))))
            ups.append(silu)
            hidden = (silu * pre_up).astype(BF16)

            @pl.when(core == h)
            def _():
                for n, sample in enumerate(((0,), range(1, SAMPLES))[part]):
                    hidden_t[sample] = lax.dot_general(
                        spread,
                        hidden[n * first_rows : (n + 1) * first_rows],
                        (((1,), (1,)), ((), ())),
                        preferred_element_type=F32,
                    ).astype(BF16)

        factor_gate[at, :] = jnp.concatenate(gates, axis=1)
        factor_up[at, :] = jnp.concatenate(ups, axis=1)

    forward_end(0)

    @pl.when(jnp.logical_not(is_top))
    def _():
        forward_end(1)

    lag = 2

    @pl.loop(0, steps)
    def _(step):
        @pl.when(jnp.logical_or(step > 0, jnp.logical_not(is_top)))
        def _():
            first(step)

        @pl.when(step >= lag)
        def _():
            third(step - lag)

        @pl.when(jnp.logical_and(is_top, step == lag))
        def _():
            forward_end(1)

        second(step)

        @pl.when(jnp.logical_and(is_top, step == lag - 1))
        def _():
            forward_start(1)

    @pl.loop(steps - lag, jnp.where(is_last, steps - lag, steps))
    def _(step):
        third(step)

    wait(w_own, load_sem.at[3])

    @pl.loop(0, steps)
    def _(step):
        wait(g_other.at[:, rows_of(step)], forward_sem.at[1, step])

    per_sample = rows // SAMPLES

    @pl.loop(0, chips // 2)
    def _(pair):
        for grads, parity in ((g_all, core), (g_other, other)):
            blocks = [2 * pair, 2 * pair + 1]
            columns = [columns_of(k, parity) for k in blocks]
            squares = None
            for sample in range(SAMPLES):
                some = jnp.concatenate(
                    [grads[k, pl.ds(sample * per_sample, per_sample), :] for k in blocks], axis=1
                )
                weight_grad = jnp.dot(hidden_t[sample], some, preferred_element_type=F32)
                square = weight_grad * weight_grad
                squares = square if squares is None else squares + square
            weight = jnp.dot(
                spread,
                jnp.concatenate([w_own[:, c] for c in columns], axis=1),
                preferred_element_type=F32,
            )
            score = jnp.abs(weight) * jnp.sqrt(squares)
            a, b, c, d = [score[i * fourth : (i + 1) * fourth] for i in range(4)]
            high_ab, low_ab = jnp.maximum(a, b), jnp.minimum(a, b)
            high_cd, low_cd = jnp.maximum(c, d), jnp.minimum(c, d)
            best = jnp.maximum(high_ab, high_cd)
            next_best = jnp.maximum(jnp.minimum(high_ab, high_cd), jnp.maximum(low_ab, low_cd))
            kept = best + next_best
            for n in range(2):
                kept_ref[:, columns[n]] = kept[:, n * CHUNK : (n + 1) * CHUNK]

    @pl.loop(jnp.where(is_last, steps - lag, steps), steps)
    def _(step):
        third(step)

    wait(both_t.at[0, core], swap_sem.at[0])
    wait(both_t.at[1, core], swap_sem.at[1])
    wait(w_down.at[core], swap_sem.at[2])
    for part, at in enumerate(parts):
        wait(x_all.at[pl.ds(0, chips - 1), at], x_sem.at[part])
        for n in range(2):
            for h in range(2):
                wait(pre_send.at[n, h, at], pre_sem.at[0, part, 2 * n + h])

    @pl.loop(0, steps)
    def _(step):
        at = rows_of(step)
        wait(part_send.at[at], part_sem.at[0, step])
        wait(g_all.at[:, at], forward_sem.at[0, step])
        wait(recv_buf.at[:, at], term_sem.at[0, step])

        @pl.when(jnp.logical_not(is_last))
        def _():
            wait(g_all.at[:, at], below_sem.at[step])

        @pl.when(is_top)
        def _():
            wait(recv_buf.at[:, at], below_sem.at[steps + step])


def hand_on(grads_in, kept_in, grads_out, kept_out):
    grads_out[...] = grads_in[...]
    kept_out[...] = kept_in[...]


def shards(sections, section_inputs, top_gradient, gate_weight, up_weight, down_weight):
    _, rows, width = section_inputs.shape
    _, model, units = gate_weight.shape
    chips = model // CHUNK // 2
    step_rows = ROWS_PER_STEP
    steps = rows // step_rows
    half = chips * CHUNK
    vmem = pl.BlockSpec(memory_space=pltpu.VMEM)
    hbm = pl.BlockSpec(memory_space=pl.ANY)
    dma = pltpu.SemaphoreType.DMA
    grads, kept = pl.pallas_call(
        functools.partial(kernel, sections, chips, rows, step_rows, units),
        out_shape=(
            jax.ShapeDtypeStruct((rows, width), F32),
            jax.ShapeDtypeStruct((units // 4, model), F32),
        ),
        in_specs=[vmem, vmem, hbm, hbm, hbm],
        out_specs=(vmem, vmem),
        scratch_shapes=[
            pltpu.VMEM((2, units, half), BF16),
            pltpu.VMEM((units, model), BF16),
            pltpu.VMEM((half, 2 * units), BF16),
            pltpu.VMEM((2, 2, units, half), BF16),
            pltpu.VMEM((chips, rows, CHUNK), BF16),
            pltpu.VMEM((chips, rows, CHUNK), BF16),
            pltpu.VMEM((chips, rows, CHUNK), BF16),
            pltpu.VMEM((rows, CHUNK), BF16),
            pltpu.VMEM((rows, CHUNK), BF16),
            pltpu.VMEM((chips, rows, CHUNK), BF16),
            pltpu.VMEM((chips - 1, rows, CHUNK), BF16),
            pltpu.VMEM((rows, 2 * units), F32),
            pltpu.VMEM((rows, 2 * units), BF16),
            pltpu.VMEM((rows, 2 * units), BF16),
            pltpu.VMEM((2, 2, rows, units), F32),
            pltpu.VMEM((2, 2, rows, units), BF16),
            pltpu.VMEM((2, 2, rows, units), BF16),
            pltpu.VMEM((rows, 2 * units), F32),
            pltpu.VMEM((rows, 2 * units), F32),
            pltpu.VMEM((SAMPLES, units, rows // SAMPLES), BF16),
            dma((4,)),
            dma((6,)),
            dma((4,)),
            dma((2, 2, 4)),
            dma((steps,)),
            dma((2 * steps,)),
            dma((2, steps)),
            dma((2, steps)),
            dma((2, steps)),
        ],
        compiler_params=pltpu.CompilerParams(
            collective_id=0, has_side_effects=True, vmem_limit_bytes=56 * 1024 * 1024
        ),
    )(
        section_inputs[0],
        top_gradient,
        gate_weight[0].T,
        up_weight[0].T,
        down_weight[0],
    )
    grads, kept = pl.pallas_call(
        hand_on,
        out_shape=(
            jax.ShapeDtypeStruct(grads.shape, F32),
            jax.ShapeDtypeStruct(kept.shape, F32),
        ),
        in_specs=[vmem, vmem],
        out_specs=(vmem, vmem),
    )(grads, kept)
    return (grads[None], kept[None])


def solution(mesh):
    in_specs = (
        P("section", None, "tp"),
        P(None, "tp"),
        P("section", None, "tp"),
        P("section", None, "tp"),
        P("section", "tp", None),
    )
    out_specs = (P("section", None, "tp"), P("section", "tp", None))
    body = functools.partial(shards, mesh.shape["section"])
    return jax.shard_map(body, mesh=mesh, in_specs=in_specs, out_specs=out_specs, check_vma=False)
```

```python
import functools

import jax
import jax.numpy as jnp
from jax import lax
from jax.experimental import pallas as pl
from jax.experimental.pallas import tpu as pltpu
from jax.sharding import PartitionSpec as P

SAMPLES = 3
CHUNK = 128
ROWS_PER_STEP = 32
MESH = pl.DeviceIdType.MESH
BF16 = jnp.bfloat16
F32 = jnp.float32


def grid_sides(chips):
    side = 1
    while side * side < chips:
        side *= 2
    return chips // side, side


def ring_distance(step, size):
    return min(step, size - step)


def chip_offsets(nx, ny):
    offsets = [(dx, dy) for dx in range(nx) for dy in range(ny)]
    return sorted(offsets, key=lambda o: -(ring_distance(o[0], nx) + ring_distance(o[1], ny)))


def kernel(
    sections,
    chips,
    rows,
    step_rows,
    units,
    x_ref,
    top_ref,
    wg_hbm,
    wu_hbm,
    wd_hbm,
    grad_ref,
    kept_ref,
    w_down,
    w_own,
    down_t,
    both_t,
    x_all,
    g_all,
    g_other,
    top16,
    result16,
    send_buf,
    recv_buf,
    part_mine,
    part_send,
    part_other,
    pre_mine,
    pre_send,
    pre_other,
    factor_gate,
    factor_up,
    hidden_t,
    load_sem,
    swap_sem,
    x_sem,
    pre_sem,
    gather_sem,
    below_sem,
    part_sem,
    forward_sem,
    term_sem,
):
    nx, ny = grid_sides(chips)
    offsets = chip_offsets(nx, ny)
    steps = rows // step_rows
    half = chips * CHUNK
    section = lax.axis_index("section")
    index = lax.axis_index("tp")
    chip, core = index // 2, lax.rem(index, 2)
    other = 1 - core
    chip_x, chip_y = chip // ny, lax.rem(chip, ny)
    places = [lax.rem(chip_x + dx, nx) * ny + lax.rem(chip_y + dy, ny) for dx, dy in offsets]
    sibling = (section, 2 * chip + other)
    above = lax.rem(section + 1, sections)
    below = lax.rem(section + sections - 1, sections)
    is_top = section == sections - 1
    is_last = section == 0

    def columns_of(place, parity):
        return pl.ds(pl.multiple_of((2 * place + parity) * CHUNK, CHUNK), CHUNK)

    for n, source in enumerate((wg_hbm, wu_hbm)):
        for t, place in enumerate(places):
            pltpu.make_async_copy(
                source.at[:, columns_of(place, core)],
                both_t.at[n, core, :, pl.ds(t * CHUNK, CHUNK)],
                load_sem.at[n],
            ).start()
    for k in range(chips):
        pltpu.make_async_copy(
            wd_hbm.at[:, columns_of(k, core)],
            w_down.at[core, :, pl.ds(k * CHUNK, CHUNK)],
            load_sem.at[2],
        ).start()
    pltpu.make_async_copy(wd_hbm, w_own, load_sem.at[3]).start()

    barrier = pltpu.get_barrier_semaphore()
    pl.semaphore_signal(barrier, inc=1, device_id=sibling, device_id_type=MESH)
    for place in places[:-1]:
        pl.semaphore_signal(
            barrier, inc=1, device_id=(section, 2 * place + core), device_id_type=MESH
        )

    @pl.when(jnp.logical_not(is_top))
    def _():
        for place in places:
            pl.semaphore_signal(
                barrier, inc=1, device_id=(above, 2 * place + core), device_id_type=MESH
            )

    @pl.when(jnp.logical_not(is_last))
    def _():
        for place in places:
            pl.semaphore_signal(
                barrier, inc=1, device_id=(below, 2 * place + core), device_id_type=MESH
            )

    top16[...] = top_ref[...].astype(BF16)
    neighbours = (
        chips
        + jnp.where(is_top, 0, chips)
        + jnp.where(is_last, 0, chips)
    )
    pl.semaphore_wait(barrier, neighbours)

    def spread_top(step):
        at = pl.ds(step * step_rows, step_rows)
        for place in places[:-1]:
            pltpu.make_async_remote_copy(
                src_ref=top16.at[at],
                dst_ref=g_all.at[chip, at],
                send_sem=below_sem.at[steps + step],
                recv_sem=gather_sem.at[step],
                device_id=(section, 2 * place + core),
                device_id_type=MESH,
            ).start()
        pltpu.make_async_copy(top16.at[at], g_all.at[chip, at], gather_sem.at[step]).start()

    first_rows = rows // SAMPLES
    parts = (pl.ds(0, first_rows), pl.ds(first_rows, rows - first_rows))

    def spread_x(part):
        at = parts[part]
        for place in places[:-1]:
            pltpu.make_async_remote_copy(
                src_ref=x_ref.at[at],
                dst_ref=x_all.at[chip, at],
                send_sem=x_sem.at[part],
                recv_sem=x_sem.at[2 + part],
                device_id=(section, 2 * place + core),
                device_id_type=MESH,
            ).start()
        pltpu.make_async_copy(x_ref.at[at], x_all.at[chip, at], x_sem.at[2 + part]).start()

    spread_x(0)

    @pl.when(is_top)
    def _():
        spread_top(0)
        spread_top(1)

    spread_x(1)

    for n, source in enumerate((wg_hbm, wu_hbm)):
        for t, place in enumerate(places):
            pltpu.make_async_remote_copy(
                src_ref=source.at[:, columns_of(place, other)],
                dst_ref=both_t.at[n, core, :, pl.ds(t * CHUNK, CHUNK)],
                send_sem=swap_sem.at[n],
                recv_sem=swap_sem.at[3 + n],
                device_id=sibling,
                device_id_type=MESH,
            ).start()
    for k in range(chips):
        pltpu.make_async_remote_copy(
            src_ref=wd_hbm.at[:, columns_of(k, other)],
            dst_ref=w_down.at[core, :, pl.ds(k * CHUNK, CHUNK)],
            send_sem=swap_sem.at[2],
            recv_sem=swap_sem.at[5],
            device_id=sibling,
            device_id_type=MESH,
        ).start()

    @pl.when(is_top)
    def _():
        for step in range(2, steps):
            spread_top(step)

    def wait(ref, sem):
        pltpu.make_async_copy(ref, ref, sem).wait()

    def forward_start(part):
        at = parts[part]
        wait(x_all.at[:, at], x_sem.at[2 + part])
        x_rows = jnp.concatenate([x_all[place, at, :] for place in places], axis=1)
        for n in range(2):
            if part == 0:
                wait(both_t.at[n, core], load_sem.at[n])
                wait(both_t.at[n, other], swap_sem.at[3 + n])
            for h in range(2):
                partial = lax.dot_general(
                    x_rows, both_t[n, h], (((1,), (1,)), ((), ())), preferred_element_type=F32
                )
                pre_mine[n, h, at, :] = partial
                pre_send[n, h, at, :] = partial.astype(BF16)
                pltpu.make_async_remote_copy(
                    src_ref=pre_send.at[n, h, at],
                    dst_ref=pre_other.at[n, h, at],
                    send_sem=pre_sem.at[0, part, 2 * n + h],
                    recv_sem=pre_sem.at[1, part, 2 * n + h],
                    device_id=sibling,
                    device_id_type=MESH,
                ).start()

    forward_start(0)

    @pl.when(jnp.logical_not(is_top))
    def _():
        forward_start(1)

    wait(w_down.at[core], load_sem.at[2])
    wait(w_down.at[other], swap_sem.at[5])
    for k in range(chips):
        at = pl.ds(k * CHUNK, CHUNK)
        down_t[at, :] = jnp.concatenate([w_down[0, :, at], w_down[1, :, at]], axis=0).T

    fourth = units // 4
    to_place = lax.broadcasted_iota(jnp.int32, (units, units), 0)
    from_unit = lax.broadcasted_iota(jnp.int32, (units, units), 1)
    member = (
        (to_place >= fourth).astype(jnp.int32)
        + (to_place >= 2 * fourth).astype(jnp.int32)
        + (to_place >= 3 * fourth).astype(jnp.int32)
    )
    spread = (from_unit == 4 * (to_place - member * fourth) + member).astype(F32).astype(BF16)

    def rows_of(step):
        return pl.ds(pl.multiple_of(step * step_rows, step_rows), step_rows)

    def first(step):
        at = rows_of(step)
        wait(g_all.at[:, at], gather_sem.at[step])
        grads = jnp.concatenate([g_all[k, at, :] for k in range(chips)], axis=1)
        partial = jnp.dot(grads, down_t[...], preferred_element_type=F32)
        part_mine[at, :] = partial
        part_send[at, :] = partial.astype(BF16)
        pltpu.make_async_remote_copy(
            src_ref=part_send.at[at],
            dst_ref=part_other.at[at],
            send_sem=part_sem.at[0, step],
            recv_sem=part_sem.at[1, step],
            device_id=sibling,
            device_id_type=MESH,
        ).start()

    def second(step):
        at = rows_of(step)
        wait(part_other.at[at], part_sem.at[1, step])
        hidden_grad = part_mine[at, :] + part_other[at, :].astype(F32)
        both = jnp.concatenate(
            [
                (hidden_grad * factor_gate[at, :]).astype(BF16),
                (hidden_grad * factor_up[at, :]).astype(BF16),
            ],
            axis=1,
        )
        for four in range(chips // 4):
            term = jnp.dot(
                both,
                both_t[:, :, :, pl.ds(4 * four * CHUNK, 4 * CHUNK)].reshape(4 * units, 4 * CHUNK),
                preferred_element_type=F32,
            ).astype(BF16)
            for t in range(4 * four, 4 * four + 4):
                send_buf[t, at, :] = term[:, (t - 4 * four) * CHUNK : (t - 4 * four + 1) * CHUNK]
                if t < chips - 1:
                    pltpu.make_async_remote_copy(
                        src_ref=send_buf.at[t, at],
                        dst_ref=recv_buf.at[t, at],
                        send_sem=term_sem.at[0, step],
                        recv_sem=term_sem.at[1, step],
                        device_id=(section, 2 * places[t] + core),
                        device_id_type=MESH,
                    ).start()

    def pass_on(step):
        at = rows_of(step)
        pltpu.make_async_remote_copy(
            src_ref=g_all.at[:, at],
            dst_ref=g_other.at[:, at],
            send_sem=forward_sem.at[0, step],
            recv_sem=forward_sem.at[1, step],
            device_id=sibling,
            device_id_type=MESH,
        ).start()

    def third(step):
        at = rows_of(step)
        wait(recv_buf.at[:, at], term_sem.at[1, step])
        total = send_buf[chips - 1, at, :].astype(F32)
        for t in range(chips - 1):
            total = total + recv_buf[t, at, :].astype(F32)
        result = jnp.where(is_top, top_ref[at, :], g_all[chip, at, :].astype(F32)) + total
        grad_ref[at, :] = result
        result16[at, :] = result.astype(BF16)

        @pl.when(jnp.logical_not(is_last))
        def _():
            for place in places:
                pltpu.make_async_remote_copy(
                    src_ref=result16.at[at],
                    dst_ref=g_all.at[chip, at],
                    send_sem=below_sem.at[step],
                    recv_sem=gather_sem.at[step],
                    device_id=(below, 2 * place + core),
                    device_id_type=MESH,
                ).start()

    @pl.when(is_top)
    def _():
        first(0)

    def forward_end(part):
        at = parts[part]
        gates, ups = [], []
        for h in range(2):
            wait(pre_other.at[0, h, at], pre_sem.at[1, part, h])
            wait(pre_other.at[1, h, at], pre_sem.at[1, part, 2 + h])
            pre_gate = pre_mine[0, h, at, :] + pre_other[0, h, at, :].astype(F32)
            pre_up = pre_mine[1, h, at, :] + pre_other[1, h, at, :].astype(F32)
            sigmoid = jax.nn.sigmoid(pre_gate)
            silu = pre_gate * sigmoid
            gates.append(pre_up * (sigmoid * (1.0 + pre_gate * (1.0 - sigmoid))))
            ups.append(silu)
            hidden = (silu * pre_up).astype(BF16)

            @pl.when(core == h)
            def _():
                for n, sample in enumerate(((0,), range(1, SAMPLES))[part]):
                    hidden_t[sample] = lax.dot_general(
                        spread,
                        hidden[n * first_rows : (n + 1) * first_rows],
                        (((1,), (1,)), ((), ())),
                        preferred_element_type=F32,
                    ).astype(BF16)

        factor_gate[at, :] = jnp.concatenate(gates, axis=1)
        factor_up[at, :] = jnp.concatenate(ups, axis=1)

    forward_end(0)

    @pl.when(jnp.logical_not(is_top))
    def _():
        forward_end(1)

    lag = 2

    @pl.loop(0, steps)
    def _(step):
        @pl.when(jnp.logical_or(step > 0, jnp.logical_not(is_top)))
        def _():
            first(step)

        @pl.when(step >= lag)
        def _():
            third(step - lag)

        @pl.when(jnp.logical_and(is_top, step == lag))
        def _():
            forward_end(1)

        second(step)
        pass_on(step)

        @pl.when(jnp.logical_and(is_top, step == lag - 1))
        def _():
            forward_start(1)

    @pl.loop(steps - lag, jnp.where(is_last, steps - lag, steps))
    def _(step):
        third(step)

    wait(w_own, load_sem.at[3])

    @pl.loop(0, steps)
    def _(step):
        wait(g_other.at[:, rows_of(step)], forward_sem.at[1, step])

    per_sample = rows // SAMPLES

    @pl.loop(0, chips // 2)
    def _(pair):
        for grads, parity in ((g_all, core), (g_other, other)):
            blocks = [2 * pair, 2 * pair + 1]
            columns = [columns_of(k, parity) for k in blocks]
            squares = None
            for sample in range(SAMPLES):
                some = jnp.concatenate(
                    [grads[k, pl.ds(sample * per_sample, per_sample), :] for k in blocks], axis=1
                )
                weight_grad = jnp.dot(hidden_t[sample], some, preferred_element_type=F32)
                square = weight_grad * weight_grad
                squares = square if squares is None else squares + square
            weight = jnp.dot(
                spread,
                jnp.concatenate([w_own[:, c] for c in columns], axis=1),
                preferred_element_type=F32,
            )
            score = jnp.abs(weight) * jnp.sqrt(squares)
            a, b, c, d = [score[i * fourth : (i + 1) * fourth] for i in range(4)]
            high_ab, low_ab = jnp.maximum(a, b), jnp.minimum(a, b)
            high_cd, low_cd = jnp.maximum(c, d), jnp.minimum(c, d)
            best = jnp.maximum(high_ab, high_cd)
            next_best = jnp.maximum(jnp.minimum(high_ab, high_cd), jnp.maximum(low_ab, low_cd))
            kept = best + next_best
            for n in range(2):
                kept_ref[:, columns[n]] = kept[:, n * CHUNK : (n + 1) * CHUNK]

    @pl.loop(jnp.where(is_last, steps - lag, steps), steps)
    def _(step):
        third(step)

    wait(both_t.at[0, core], swap_sem.at[0])
    wait(both_t.at[1, core], swap_sem.at[1])
    wait(w_down.at[core], swap_sem.at[2])
    for part, at in enumerate(parts):
        wait(x_all.at[pl.ds(0, chips - 1), at], x_sem.at[part])
        for n in range(2):
            for h in range(2):
                wait(pre_send.at[n, h, at], pre_sem.at[0, part, 2 * n + h])

    @pl.loop(0, steps)
    def _(step):
        at = rows_of(step)
        wait(part_send.at[at], part_sem.at[0, step])
        wait(g_all.at[:, at], forward_sem.at[0, step])
        wait(recv_buf.at[:, at], term_sem.at[0, step])

        @pl.when(jnp.logical_not(is_last))
        def _():
            wait(g_all.at[:, at], below_sem.at[step])

        @pl.when(is_top)
        def _():
            wait(recv_buf.at[:, at], below_sem.at[steps + step])


def hand_on(grads_in, kept_in, grads_out, kept_out):
    grads_out[...] = grads_in[...]
    kept_out[...] = kept_in[...]


def shards(sections, section_inputs, top_gradient, gate_weight, up_weight, down_weight):
    _, rows, width = section_inputs.shape
    _, model, units = gate_weight.shape
    chips = model // CHUNK // 2
    step_rows = ROWS_PER_STEP
    steps = rows // step_rows
    half = chips * CHUNK
    vmem = pl.BlockSpec(memory_space=pltpu.VMEM)
    hbm = pl.BlockSpec(memory_space=pl.ANY)
    dma = pltpu.SemaphoreType.DMA
    grads, kept = pl.pallas_call(
        functools.partial(kernel, sections, chips, rows, step_rows, units),
        out_shape=(
            jax.ShapeDtypeStruct((rows, width), F32),
            jax.ShapeDtypeStruct((units // 4, model), F32),
        ),
        in_specs=[vmem, vmem, hbm, hbm, hbm],
        out_specs=(vmem, vmem),
        scratch_shapes=[
            pltpu.VMEM((2, units, half), BF16),
            pltpu.VMEM((units, model), BF16),
            pltpu.VMEM((half, 2 * units), BF16),
            pltpu.VMEM((2, 2, units, half), BF16),
            pltpu.VMEM((chips, rows, CHUNK), BF16),
            pltpu.VMEM((chips, rows, CHUNK), BF16),
            pltpu.VMEM((chips, rows, CHUNK), BF16),
            pltpu.VMEM((rows, CHUNK), BF16),
            pltpu.VMEM((rows, CHUNK), BF16),
            pltpu.VMEM((chips, rows, CHUNK), BF16),
            pltpu.VMEM((chips - 1, rows, CHUNK), BF16),
            pltpu.VMEM((rows, 2 * units), F32),
            pltpu.VMEM((rows, 2 * units), BF16),
            pltpu.VMEM((rows, 2 * units), BF16),
            pltpu.VMEM((2, 2, rows, units), F32),
            pltpu.VMEM((2, 2, rows, units), BF16),
            pltpu.VMEM((2, 2, rows, units), BF16),
            pltpu.VMEM((rows, 2 * units), F32),
            pltpu.VMEM((rows, 2 * units), F32),
            pltpu.VMEM((SAMPLES, units, rows // SAMPLES), BF16),
            dma((4,)),
            dma((6,)),
            dma((4,)),
            dma((2, 2, 4)),
            dma((steps,)),
            dma((2 * steps,)),
            dma((2, steps)),
            dma((2, steps)),
            dma((2, steps)),
        ],
        compiler_params=pltpu.CompilerParams(
            collective_id=0, has_side_effects=True, vmem_limit_bytes=56 * 1024 * 1024
        ),
    )(
        section_inputs[0],
        top_gradient,
        gate_weight[0].T,
        up_weight[0].T,
        down_weight[0],
    )
    grads, kept = pl.pallas_call(
        hand_on,
        out_shape=(
            jax.ShapeDtypeStruct(grads.shape, F32),
            jax.ShapeDtypeStruct(kept.shape, F32),
        ),
        in_specs=[vmem, vmem],
        out_specs=(vmem, vmem),
    )(grads, kept)
    return (grads[None], kept[None])


def solution(mesh):
    in_specs = (
        P("section", None, "tp"),
        P(None, "tp"),
        P("section", None, "tp"),
        P("section", None, "tp"),
        P("section", "tp", None),
    )
    out_specs = (P("section", None, "tp"), P("section", "tp", None))
    body = functools.partial(shards, mesh.shape["section"])
    return jax.shard_map(body, mesh=mesh, in_specs=in_specs, out_specs=out_specs, check_vma=False)
```
